32 devices in a mesh: mesh: 4 (over y, x), mode: 8 (over z, core).
Axes of the slice: x: 2, y: 2, z: 4, core: 2. Of those that a mesh axis runs over, the one named last changes fastest.
Arguments:
- magnetic: float32 [2, 6, 64, 8192], P(None, None, 'mode', 'mesh'), may hold values from -6 to 6
- velocity: float32 [3, 128, 8192], P(None, None, ('mesh', 'mode')), may hold values from -3 to 3
- stiffness: float32 [6, 6, 4096], P(None, None, 'mesh')
- mass_r: float32 [6, 6, 4096], P(None, None, 'mesh')
- coupling: float32 [6, 6, 4096], P(None, None, 'mesh'), may hold values from -3 to 3
- inv_mass: float32 [8192], P('mesh'), may hold values from 0.5 to 2
- connect: int32 [6, 4096], P(None, 'mesh'), may hold values from 0 to 2559, as said below
- interface: int32 [4, 512], P('mesh'), may hold values from 0 to 2047, as said below
- counts: int32 [4, 2], P('mesh'), may hold values from 0 to 256, as said below
- elem_live: int32 [4], P('mesh'), may hold values from 128 to 1024
Outputs:
- advanced: float32 [2, 6, 64, 8192], P(None, None, 'mode', 'mesh')
The draws below stay inside these ranges and needn't reach their ends.
Inputs may be any that keep to these rules, and one draw needn't show every extreme that they name: `connect`: entries below 2048 are the partition's own nodes; 2048 + s appears only for s < counts[q - 1, 1] and 2304 + s only for s < counts[q + 1, 0]. `interface`: each row holds distinct node indices of its partition; the first counts[q, 0] are shared with partition q - 1, the next counts[q, 1] with partition q + 1. counts[0, 0] = 0 and counts[3, 1] = 0.
All inputs are finite; a program needn't handle non-finite values.
Results may differ from the reference program's by a relative error of at most 0.00005.
Values sent between devices are 32-bit elements; how exact they have to be, the bound alone decides.
No kernel may reach another device: no remote copies, remote signals or barrier semaphores. Data moves between devices by JAX's collectives and lax.ppermute only.
A program may use at most 320 MiB of HBM per device.

```python
import math
import jax
import jax.numpy as jnp
from jax import lax

MODES = 64
POINTS = 128
NODE_DEV = 2048
CAP = 256
ELEM_DEV = 1024
NODES = 8192
ELEMS = 4096
N_MESH = 4


def interface_counts(key):
    base_key = jax.random.fold_in(key, 7001)
    drawn_sizes = jax.random.randint(base_key, (N_MESH, 2), CAP // 4, CAP + 1)
    full_right = jax.random.randint(jax.random.fold_in(base_key, 1), (), 0, N_MESH - 1)
    full_left = jax.random.randint(jax.random.fold_in(base_key, 2), (), 1, N_MESH)
    rank_ids = jnp.arange(N_MESH)
    left_sizes = jnp.where(rank_ids == full_left, CAP, drawn_sizes[:, 0])
    left_sizes = jnp.where(rank_ids == 0, 0, left_sizes)
    right_sizes = jnp.where(rank_ids == full_right, CAP, drawn_sizes[:, 1])
    right_sizes = jnp.where(rank_ids == N_MESH - 1, 0, right_sizes)
    return (jnp.stack([left_sizes, right_sizes], 1).astype(jnp.int32), full_left)


def element_block(key, diag_top, offdiag):
    unit = jnp.eye(6, dtype=jnp.float32)[:, :, None]
    diagonal = jnp.exp(jax.random.uniform(key, (6, 1, ELEM_DEV * N_MESH), jnp.float32, 0.0, math.log(diag_top)))
    return unit * diagonal + (1.0 - unit) * offdiag


def draw_stiffness(key, part):
    key = jax.random.fold_in(key, 3)
    shape_all = (6, 6, ELEM_DEV * N_MESH)
    offdiag = 0.5 * jax.random.normal(jax.random.fold_in(key, 1), shape_all, jnp.float32)
    return element_block(jax.random.fold_in(key, 2), 8.0, offdiag)


def draw_mass_r(key, part):
    key = jax.random.fold_in(key, 5)
    shape_all = (6, 6, ELEM_DEV * N_MESH)
    offdiag = 0.5 * jax.random.normal(jax.random.fold_in(key, 1), shape_all, jnp.float32)
    return 0.0005 * element_block(jax.random.fold_in(key, 2), 8.0, offdiag)


def draw_connect(key, part):
    sizes_all, full_left = interface_counts(key)
    key = jax.random.fold_in(key, 11)
    nothing = jnp.zeros((1,), jnp.int32)
    ghost_left = jnp.concatenate([nothing, sizes_all[:-1, 1]])
    ghost_right = jnp.concatenate([sizes_all[1:, 0], nothing])
    span_all = (NODE_DEV + ghost_left + ghost_right)[None, :, None]
    drawn_ids = jax.random.randint(key, (6, N_MESH, ELEM_DEV), 0, span_all)
    shifted = ghost_left[None, :, None]
    local_ids = jnp.where(drawn_ids < NODE_DEV + shifted, drawn_ids, drawn_ids - shifted + CAP)
    corner = jnp.arange(6)[:, None, None]
    owner_ids = jnp.arange(N_MESH)[None, :, None]
    element = jnp.arange(ELEM_DEV)[None, None, :]
    first_elem = (owner_ids == full_left - 1) & (element == 0)
    local_ids = jnp.where(first_elem & (corner == 0), NODE_DEV + 2 * CAP - 1, local_ids)
    local_ids = jnp.where(first_elem & (corner == 1), 0, local_ids)
    return local_ids.reshape(6, N_MESH * ELEM_DEV).astype(jnp.int32)


def draw_interface(key, part):
    key = jax.random.fold_in(key, 13)
    row_keys = jax.random.split(key, N_MESH)
    return jax.vmap(lambda row_key: jax.random.permutation(row_key, NODE_DEV)[:2 * CAP])(row_keys).astype(jnp.int32)


def draw_counts(key, part):
    return interface_counts(key)[0]


def draw_elem_live(key, part):
    key = jax.random.fold_in(key, 17)
    drawn_sizes = jax.random.randint(key, (N_MESH,), ELEM_DEV // 8, ELEM_DEV + 1)
    full_rank = jax.random.randint(jax.random.fold_in(key, 1), (), 0, N_MESH)
    return jnp.where(jnp.arange(N_MESH) == full_rank, ELEM_DEV, drawn_sizes).astype(jnp.int32)


def steps_of(key, shape, shards, smallest, top_value):
    level = 1.0
    for axis_at, blocks in shards:
        steps = jax.random.uniform(jax.random.fold_in(jax.random.fold_in(key, 6), axis_at), (blocks,), jnp.float32, smallest / len(shards), top_value / len(shards))
        level = level * jnp.repeat(jnp.exp(steps), shape[axis_at] // blocks).reshape((-1,) + (1,) * (len(shape) - 1 - axis_at))
    return level


def bell_draw(stream_key, dims, width, bound, cuts=(), kind=jnp.bfloat16):
    drawn = jax.random.normal(stream_key, dims, jnp.float32) * width
    if len(cuts) > 0:
        drawn = steps_of(stream_key, dims, cuts, -0.22, 0.18) * drawn
    return jnp.clip(drawn, min=-bound, max=bound).astype(kind)


def setup_inputs(seed: int = 0) -> dict:
    seeds = jax.random.split(jax.random.key(seed), 11)
    return {
        "magnetic": bell_draw(seeds[0], (2, 6, MODES, NODES), 1.0, 6.0, ((2, 8), (3, 4)), jnp.float32),
        "velocity": bell_draw(seeds[1], (3, POINTS, NODES), 0.5, 3.0, ((2, 32),), jnp.float32),
        "stiffness": draw_stiffness(jax.random.fold_in(seeds[10], 71), 0),
        "mass_r": draw_mass_r(jax.random.fold_in(seeds[10], 71), 0),
        "coupling": bell_draw(seeds[4], (6, 6, ELEMS), 0.5, 3.0, ((2, 4),), jnp.float32),
        "inv_mass": jnp.clip(jnp.exp(math.log(2.0) - 1.3862944 * jax.random.uniform(seeds[5], (NODES,), jnp.float32) ** steps_of(seeds[5], (NODES,), ((0, 4),), -0.2, 0.2)), 0.5, 2.0),
        "connect": draw_connect(jax.random.fold_in(seeds[10], 71), 0),
        "interface": draw_interface(jax.random.fold_in(seeds[10], 71), 0),
        "counts": draw_counts(jax.random.fold_in(seeds[10], 71), 0),
        "elem_live": draw_elem_live(jax.random.fold_in(seeds[10], 71), 0),
    }


diffusivity = 1.0
time_step = 0.1
highest = lax.Precision.HIGHEST


def transform_tables(spectral_modes):
    samples = 2 * spectral_modes
    sample_ids = jnp.arange(samples)[:, None]
    mode_ids = jnp.arange(spectral_modes)[None, :]
    phases = (2.0 * math.pi / samples) * ((sample_ids * mode_ids) % samples).astype(jnp.float32)
    cosines = jnp.cos(phases)
    sines = jnp.sin(phases)
    inverse_fourier = jnp.concatenate([cosines, sines], 1)
    weights = jnp.where(mode_ids == 0, 1.0, 2.0).astype(jnp.float32) / samples
    forward_fourier = jnp.concatenate([(cosines * weights).T, (sines * (2.0 / samples)).T], 0)
    return inverse_fourier, forward_fourier


def electric_spectral(split_into_slabs, velocity, inverse_fourier, forward_fourier):
    group_members, vector_parts, spectral_modes, slab_width = split_into_slabs.shape
    mode_coefficient_values = split_into_slabs.reshape(group_members, 3, 2 * spectral_modes, slab_width)
    points = jnp.einsum("pc,ficn->fipn", inverse_fourier, mode_coefficient_values, precision=highest)
    vel_r, vel_t, vel_z = velocity[0], velocity[1], velocity[2]
    mag_r, mag_t, mag_z = points[:, 0], points[:, 1], points[:, 2]
    cross = jnp.stack([vel_t * mag_z - vel_z * mag_t, vel_z * mag_r - vel_r * mag_z, vel_r * mag_t - vel_t * mag_r], 1)
    back = jnp.einsum("cp,fipn->ficn", forward_fourier, cross, precision=highest)
    return back.reshape(group_members, vector_parts, spectral_modes, slab_width)


def element_terms(mag_ext, ele_ext, connect, stiffness, mass_r, coupling, mode_ids, live):
    squares = (mode_ids.astype(jnp.float32) ** 2)[:, None, None, None]
    operator = stiffness[None] + squares * mass_r[None]
    terms = jnp.zeros(mag_ext.shape[:3] + connect.shape, jnp.float32)
    for corner in range(6):
        mag_col = jnp.take(mag_ext, connect[corner], axis=3)[:, :, :, None, :]
        ele_col = jnp.take(ele_ext, connect[corner], axis=3)[:, :, :, None, :]
        terms = terms + coupling[:, corner, :][None, None, None] * ele_col
        terms = terms - diffusivity * (operator[:, :, corner, :][None, None] * mag_col)
    return jnp.where(live, terms, 0.0)


def reference(magnetic, velocity, stiffness, mass_r, coupling, inv_mass, connect, interface, counts, elem_live):
    inverse_fourier, forward_fourier = transform_tables(MODES)
    field_blocks = magnetic.reshape(2, 6, MODES, N_MESH, NODE_DEV).transpose(3, 0, 1, 2, 4)
    vel_blocks = velocity.reshape(3, POINTS, N_MESH, NODE_DEV).transpose(2, 0, 1, 3)
    electric = lax.map(lambda blocks: electric_spectral(blocks[0], blocks[1], inverse_fourier, forward_fourier), (field_blocks, vel_blocks))
    electric = electric.transpose(1, 2, 3, 0, 4).reshape(2, 6, MODES, NODES)
    slot_ids = jnp.arange(CAP, dtype=jnp.int32)
    mode_ids = jnp.arange(MODES, dtype=jnp.int32)
    assembled = jnp.zeros(magnetic.shape, jnp.float32)
    for part_id in range(N_MESH):
        own_ids = part_id * NODE_DEV + jnp.arange(NODE_DEV, dtype=jnp.int32)
        if part_id > 0:
            left_ids = (part_id - 1) * NODE_DEV + jnp.take(interface[part_id - 1], (counts[part_id - 1, 0] + slot_ids).astype(jnp.int32))
        else:
            left_ids = jnp.zeros((CAP,), jnp.int32)
        if part_id < N_MESH - 1:
            right_ids = (part_id + 1) * NODE_DEV + jnp.take(interface[part_id + 1], slot_ids)
        else:
            right_ids = jnp.zeros((CAP,), jnp.int32)
        node_map = jnp.concatenate([own_ids, left_ids.astype(jnp.int32), right_ids.astype(jnp.int32)])
        lower = part_id * ELEM_DEV
        local_conn = connect[:, lower:lower + ELEM_DEV]
        global_conn = jnp.take(node_map, local_conn).astype(jnp.int32)
        live = jnp.arange(ELEM_DEV) < elem_live[part_id]
        terms = element_terms(magnetic, electric, global_conn, stiffness[:, :, lower:lower + ELEM_DEV], mass_r[:, :, lower:lower + ELEM_DEV], coupling[:, :, lower:lower + ELEM_DEV], mode_ids, live)
        assembled = assembled.at[:, :, :, global_conn].add(terms)
    return magnetic + time_step * inv_mass * assembled
```

```python
import functools
import math

import jax
import jax.numpy as jnp
from jax import lax
from jax.experimental import pallas as pl
from jax.experimental.pallas import tpu as pltpu
from jax.sharding import PartitionSpec as P

diffusivity = 1.0
time_step = 0.1
f32 = jnp.float32
bf16 = jnp.bfloat16
KERNEL_VMEM = 30 << 20
ELEM_TILE = 256


def whole_block(shape):
    return pl.BlockSpec(shape, lambda *ids: (0,) * len(shape))


def params():
    return pltpu.CompilerParams(vmem_limit_bytes=KERNEL_VMEM)


def cost(us):
    return pl.CostEstimate(flops=0, bytes_accessed=int(us * 3.0e6), transcendentals=0)


def split_rows(value):
    high = value.astype(bf16)
    low = (value - high.astype(f32)).astype(bf16)
    return jnp.concatenate([high, low], 0)


def halves_sum(value):
    rows = value.shape[0] // 2
    return value[:rows] + value[rows:]


def one_hot(iota, ids):
    return jnp.where(iota == ids, 1.0, 0.0).astype(bf16)


def transform_tables(mode_dev, members, me):
    spectral_modes = mode_dev * members
    samples = 2 * spectral_modes
    row = jnp.arange(samples)
    step = row // (2 * mode_dev)
    parity = (row // mode_dev) % 2
    mode = (me ^ step) * mode_dev + row % mode_dev
    sample_ids = jnp.arange(samples)
    phases = (2.0 * math.pi / samples) * ((sample_ids[:, None] * mode[None, :]) % samples).astype(f32)
    inverse = jnp.where(parity[None, :] == 0, jnp.cos(phases), jnp.sin(phases))
    weights = jnp.where((mode == 0) & (parity == 0), 1.0, 2.0).astype(f32) / samples
    forward = (inverse * weights[None, :]).T
    return inverse, forward


def spread_table(table):
    high = table.astype(bf16)
    low = (table - high.astype(f32)).astype(bf16)
    return jnp.concatenate([high, high, low], 1)


def spread_value(value):
    high = value.astype(bf16)
    low = (value - high.astype(f32)).astype(bf16)
    return jnp.concatenate([high, low, high], 0)


def transform_kernel(members, mode_dev, fields, *refs):
    inverse, forward, velocity = refs[:3]
    blocks = refs[3 : 3 + members]
    outs = refs[3 + members :]
    pair = 2 * mode_dev
    to_points, to_modes = spread_table(inverse[...]), spread_table(forward[...])
    for field in range(fields):
        points = []
        for part in range(3):
            low = (field * 3 + part) * pair
            stacked = jnp.concatenate([block[low : low + pair, :] for block in blocks], 0)
            points.append(
                jnp.dot(to_points, spread_value(stacked), preferred_element_type=f32)
            )
        for part in range(3):
            after, last = (part + 1) % 3, (part + 2) % 3
            cross = velocity[after] * points[last] - velocity[last] * points[after]
            back = jnp.dot(to_modes, spread_value(cross), preferred_element_type=f32)
            low = (field * 3 + part) * pair
            for step in range(members):
                outs[step][low : low + pair, :] = back[step * pair : (step + 1) * pair]


def transform(blocks, velocity, inverse, forward, mode_dev, fields):
    members = len(blocks)
    return pl.pallas_call(
        functools.partial(transform_kernel, members, mode_dev, fields),
        out_shape=[jax.ShapeDtypeStruct(block.shape, f32) for block in blocks],
        compiler_params=params(),
        cost_estimate=cost(3),
        name="transform",
    )(inverse, forward, velocity, *blocks)


def interface_kernel(count, bases, ids, *refs):
    blocks = refs[:count]
    left, right, hot = refs[count:]
    width = ids.shape[1]
    row = 0
    stacked = []
    for at, block in enumerate(blocks):
        size = block.shape[1]
        iota = lax.broadcasted_iota(jnp.int32, (size, width), 0)
        hot[row : row + size, :] = one_hot(iota, ids[...] - bases[at])
        stacked.append(split_rows(block[...]))
        row += size
    values = jnp.concatenate(stacked, 1)
    got = halves_sum(jnp.dot(values, hot[...], preferred_element_type=f32))
    left[...] = got[:, : width // 2]
    right[...] = got[:, width // 2 :]


def interface_values(blocks, bases, ids, us):
    rows = blocks[0].shape[0]
    total = sum(block.shape[1] for block in blocks)
    cap = ids.shape[1] // 2
    vmem = pl.BlockSpec(memory_space=pltpu.VMEM)
    return pl.pallas_call(
        functools.partial(interface_kernel, len(blocks)),
        in_specs=[pl.BlockSpec(memory_space=pltpu.SMEM), vmem] + [vmem] * len(blocks),
        out_shape=[jax.ShapeDtypeStruct((rows, cap), f32)] * 2,
        scratch_shapes=[pltpu.VMEM((total, 2 * cap), bf16)],
        compiler_params=params(),
        cost_estimate=cost(us),
        name="interface_values",
    )(bases, ids, *blocks)


def fill_gather(hot, conn, blocks, bases, tile):
    row = 0
    for at, block in enumerate(blocks):
        size = block.shape[1]
        iota = lax.broadcasted_iota(jnp.int32, (size, tile), 0)
        for corner in range(6):
            hot[row : row + size, corner * tile : (corner + 1) * tile] = one_hot(
                iota, conn[corner : corner + 1, :] - bases[at]
            )
        row += size


def fill_values(values, blocks):
    column = 0
    for block in blocks:
        size = block.shape[1]
        values[:, column : column + size] = split_rows(block[...])
        column += size


def magnetic_terms_kernel(count, bases, conn, stiffness, mass_r, squares, *refs):
    blocks = refs[:count]
    out, values, hot, operator = refs[count:]
    tile = conn.shape[1]

    @pl.when(pl.program_id(0) == 0)
    def _():
        fill_values(values, blocks)

    fill_gather(hot, conn, blocks, bases, tile)
    got = halves_sum(jnp.dot(values[...], hot[...], preferred_element_type=f32))
    for a in range(6):
        for b in range(6):
            operator[a * 6 + b] = diffusivity * (
                stiffness[a, b : b + 1, :] + squares[...] * mass_r[a, b : b + 1, :]
            )
    for low in range(0, out.shape[0], 8):
        for a in range(6):
            total = None
            for b in range(6):
                term = operator[a * 6 + b] * got[low : low + 8, b * tile : (b + 1) * tile]
                total = term if total is None else total + term
            out[low : low + 8, a * tile : (a + 1) * tile] = total


def magnetic_terms(blocks, bases, conn, stiffness, mass_r, squares):
    rows = blocks[0].shape[0]
    elems = conn.shape[1]
    tile = ELEM_TILE
    total = sum(block.shape[1] for block in blocks)
    elem_block = pl.BlockSpec((6, 6, tile), lambda j: (0, 0, j))
    return pl.pallas_call(
        functools.partial(magnetic_terms_kernel, len(blocks)),
        grid=(elems // tile,),
        in_specs=[
            pl.BlockSpec(memory_space=pltpu.SMEM),
            pl.BlockSpec((6, tile), lambda j: (0, j)),
            elem_block,
            elem_block,
            whole_block((8, 1)),
        ]
        + [whole_block(block.shape) for block in blocks],
        out_specs=pl.BlockSpec((rows, 6 * tile), lambda j: (0, j)),
        out_shape=jax.ShapeDtypeStruct((rows, 6 * elems), f32),
        scratch_shapes=[
            pltpu.VMEM((2 * rows, total), bf16),
            pltpu.VMEM((total, 6 * tile), bf16),
            pltpu.VMEM((36, 8, tile), f32),
        ],
        compiler_params=params(),
        cost_estimate=cost(14),
        name="magnetic_terms",
    )(bases, conn, stiffness, mass_r, squares, *blocks)


def gather_kernel(count, adds, bases, conn, *refs):
    blocks = refs[:count]
    refs = refs[count:]
    if adds:
        earlier, refs = refs[0], refs[1:]
    out, values, hot = refs
    tile = conn.shape[1]

    @pl.when(pl.program_id(0) == 0)
    def _():
        fill_values(values, blocks)

    fill_gather(hot, conn, blocks, bases, tile)
    got = halves_sum(jnp.dot(values[...], hot[...], preferred_element_type=f32))
    out[...] = got + earlier[...] if adds else got


def gathered(blocks, bases, conn, earlier, us):
    rows = blocks[0].shape[0]
    elems = conn.shape[1]
    tile = ELEM_TILE
    total = sum(block.shape[1] for block in blocks)
    wide = pl.BlockSpec((rows, 6 * tile), lambda j: (0, j))
    adds = earlier is not None
    return pl.pallas_call(
        functools.partial(gather_kernel, len(blocks), adds),
        grid=(elems // tile,),
        in_specs=[
            pl.BlockSpec(memory_space=pltpu.SMEM),
            pl.BlockSpec((6, tile), lambda j: (0, j)),
        ]
        + [whole_block(block.shape) for block in blocks]
        + [wide] * adds,
        out_specs=wide,
        out_shape=jax.ShapeDtypeStruct((rows, 6 * elems), f32),
        scratch_shapes=[
            pltpu.VMEM((2 * rows, total), bf16),
            pltpu.VMEM((total, 6 * tile), bf16),
        ],
        compiler_params=params(),
        cost_estimate=cost(us),
        name="gathered",
    )(bases, conn, *blocks, *([earlier] * adds))


def fill_scatter(hot, conn_columns, first, tile):
    iota = lax.broadcasted_iota(jnp.int32, (tile, hot.shape[1]), 1)
    for corner in range(6):
        hot[corner * tile : (corner + 1) * tile, :] = one_hot(
            iota, conn_columns[:, corner : corner + 1] - first
        )


def ghost_terms_kernel(
    first, conn, conn_columns, coupling, magnetic_part, electric_part, left, right,
    terms, sums, values, hot, hot_columns, total_sums
):
    step = pl.program_id(0)
    tile = conn.shape[1]
    cap = left.shape[1]

    @pl.when(step == 0)
    def _():
        fill_values(values, (left, right))
        total_sums[...] = jnp.zeros_like(total_sums)

    fill_gather(hot, conn, (left, right), (first, first + cap), tile)
    got = electric_part[...] + halves_sum(
        jnp.dot(values[...], hot[...], preferred_element_type=f32)
    )
    rows = got.shape[0]
    for low in range(0, rows, 16):
        for a in range(6):
            at = slice(a * tile, (a + 1) * tile)
            total = -magnetic_part[low : low + 16, at]
            for b in range(6):
                total = total + coupling[a, b : b + 1, :] * got[low : low + 16, b * tile : (b + 1) * tile]
            high = total.astype(bf16)
            terms[low : low + 16, at] = high
            terms[rows + low : rows + low + 16, at] = (total - high.astype(f32)).astype(bf16)
    fill_scatter(hot_columns, conn_columns, first, tile)
    total_sums[...] += halves_sum(
        jnp.dot(terms[...], hot_columns[...], preferred_element_type=f32)
    )

    @pl.when(step == pl.num_programs(0) - 1)
    def _():
        sums[0] = total_sums[:, :cap]
        sums[1] = total_sums[:, cap:]


def ghost_terms(first, conn, conn_columns, coupling, magnetic_part, electric_part, left, right):
    rows, cap = left.shape
    elems = conn.shape[1]
    tile = ELEM_TILE
    wide = pl.BlockSpec((rows, 6 * tile), lambda j: (0, j))
    return pl.pallas_call(
        functools.partial(ghost_terms_kernel, first),
        grid=(elems // tile,),
        in_specs=[
            pl.BlockSpec((6, tile), lambda j: (0, j)),
            pl.BlockSpec((tile, 6), lambda j: (j, 0)),
            pl.BlockSpec((6, 6, tile), lambda j: (0, 0, j)),
            wide,
            wide,
            whole_block((rows, cap)),
            whole_block((rows, cap)),
        ],
        out_specs=[
            pl.BlockSpec((2 * rows, 6 * tile), lambda j: (0, j)),
            whole_block((2, rows, cap)),
        ],
        out_shape=[
            jax.ShapeDtypeStruct((2 * rows, 6 * elems), bf16),
            jax.ShapeDtypeStruct((2, rows, cap), f32),
        ],
        scratch_shapes=[
            pltpu.VMEM((2 * rows, 2 * cap), bf16),
            pltpu.VMEM((2 * cap, 6 * tile), bf16),
            pltpu.VMEM((6 * tile, 2 * cap), bf16),
            pltpu.VMEM((rows, 2 * cap), f32),
        ],
        compiler_params=params(),
        cost_estimate=cost(8),
        name="ghost_terms",
    )(conn, conn_columns, coupling, magnetic_part, electric_part, left, right)


def own_sums_kernel(conn_columns, terms, out, hot):
    @pl.when(pl.program_id(0) == 0)
    def _():
        out[...] = jnp.zeros_like(out)

    fill_scatter(hot, conn_columns, 0, conn_columns.shape[0])
    out[...] += halves_sum(jnp.dot(terms[...], hot[...], preferred_element_type=f32))


def own_sums(conn_columns, terms, nodes):
    rows = terms.shape[0] // 2
    tile = ELEM_TILE
    elems = conn_columns.shape[0]
    return pl.pallas_call(
        own_sums_kernel,
        grid=(elems // tile,),
        in_specs=[
            pl.BlockSpec((tile, 6), lambda j: (j, 0)),
            pl.BlockSpec((2 * rows, 6 * tile), lambda j: (0, j)),
        ],
        out_specs=whole_block((rows, nodes)),
        out_shape=jax.ShapeDtypeStruct((rows, nodes), f32),
        scratch_shapes=[pltpu.VMEM((6 * tile, nodes), bf16)],
        compiler_params=params(),
        cost_estimate=cost(9),
        name="own_sums",
    )(conn_columns, terms)


def finish_kernel(columns, magnetic, sums, left, right, inv_mass, out):
    width = columns.shape[0]
    nodes = out.shape[1]
    iota = lax.broadcasted_iota(jnp.int32, (width, nodes), 1)
    hot = one_hot(iota, columns[...])
    values = jnp.concatenate([split_rows(left[...]), split_rows(right[...])], 1)
    extra = halves_sum(jnp.dot(values, hot, preferred_element_type=f32))
    out[...] = magnetic[...] + time_step * inv_mass[...] * (sums[...] + extra)


def finish(columns, magnetic, sums, left, right, inv_mass):
    return pl.pallas_call(
        finish_kernel,
        out_shape=jax.ShapeDtypeStruct(magnetic.shape, f32),
        compiler_params=params(),
        cost_estimate=cost(3),
        name="finish",
    )(columns, magnetic, sums, left, right, inv_mass)


def exchange(blocks):
    members = len(blocks)
    return [blocks[0]] + [
        lax.ppermute(blocks[s], "mode", [(k, k ^ s) for k in range(members)])
        for s in range(1, members)
    ]


def neighbours(to_left, to_right):
    count = lax.axis_size("mesh")
    from_left = lax.ppermute(to_right, "mesh", [(i, i + 1) for i in range(count - 1)])
    from_right = lax.ppermute(to_left, "mesh", [(i + 1, i) for i in range(count - 1)])
    return from_left, from_right


def on_device(
    magnetic, velocity, stiffness, mass_r, coupling, inv_mass, connect, interface, counts, elem_live
):
    fields, vector_parts, mode_dev, node_dev = magnetic.shape
    rows = fields * vector_parts * mode_dev
    cap = interface.shape[1] // 2
    elems = connect.shape[1]
    members = lax.axis_size("mode")
    me = lax.axis_index("mode")
    slab = node_dev // members
    values = magnetic.reshape(rows, node_dev)

    slabs = [
        lax.dynamic_slice_in_dim(values, (me ^ s) * slab, slab, axis=1) for s in range(members)
    ]
    arrived = exchange(slabs)

    right_nodes = lax.dynamic_slice_in_dim(interface[0], counts[0, 0], cap)
    nodes = jnp.concatenate([interface[0, :cap], right_nodes])
    node_row = nodes[None, :]
    node_column = nodes[:, None]
    live = jnp.arange(elems) < elem_live[0]
    conn = jnp.where(live, connect, -1)
    conn_columns = conn.T
    mode_ids = me * mode_dev + jnp.arange(8) % mode_dev
    squares = (mode_ids.astype(f32) ** 2)[:, None]

    zero = jnp.zeros((1,), jnp.int32)
    mag_left, mag_right = neighbours(*interface_values([values], zero, node_row, 3))
    ghost_bases = jnp.array([0, node_dev, node_dev + cap], jnp.int32)
    magnetic_part = magnetic_terms(
        [values, mag_left, mag_right], ghost_bases, conn, stiffness, mass_r, squares
    )

    inverse, forward = transform_tables(mode_dev, members, me)
    electric = exchange(transform(arrived, velocity, inverse, forward, mode_dev, fields))
    bases = (me ^ jnp.arange(members, dtype=jnp.int32)) * slab
    near = members // 2
    electric_part = gathered(electric[:near], bases[:near], conn, None, 6)
    ele_left, ele_right = neighbours(*interface_values(electric, bases, node_row, 3))
    electric_part = gathered(electric[near:], bases[near:], conn, electric_part, 6)
    terms, ghost_sums = ghost_terms(
        node_dev, conn, conn_columns, coupling, magnetic_part, electric_part, ele_left, ele_right
    )
    sum_left, sum_right = neighbours(ghost_sums[0], ghost_sums[1])
    sums = own_sums(conn_columns, terms, node_dev)
    out = finish(node_column, values, sums, sum_left, sum_right, inv_mass[None, :])
    return out.reshape(magnetic.shape)


def solution(mesh):
    return jax.shard_map(
        on_device,
        mesh=mesh,
        in_specs=(
            P(None, None, "mode", "mesh"),
            P(None, None, ("mesh", "mode")),
            P(None, None, "mesh"),
            P(None, None, "mesh"),
            P(None, None, "mesh"),
            P("mesh"),
            P(None, "mesh"),
            P("mesh", None),
            P("mesh", None),
            P("mesh"),
        ),
        out_specs=P(None, None, "mode", "mesh"),
        check_vma=False,
    )
```

```python
import functools
import math

import jax
import jax.numpy as jnp
import numpy as np
from jax import lax
from jax.experimental import pallas as pl
from jax.experimental.pallas import tpu as pltpu
from jax.sharding import PartitionSpec as P

diffusivity = 1.0
time_step = 0.1
f32 = jnp.float32
bf16 = jnp.bfloat16
KERNEL_VMEM = 20 << 20
ELEM_TILE = 256


def whole_block(shape):
    return pl.BlockSpec(shape, lambda *ids: (0,) * len(shape))


class Block:
    def __init__(self, array, rows, at=0):
        self.array, self.rows, self.at = array, rows, at
        self.shape = (rows, array.shape[1])

    def spec(self):
        at = self.at
        return pl.BlockSpec(self.shape, lambda *ids: (at, 0))


def specs(blocks):
    return [block.spec() for block in blocks]


def arrays(blocks):
    return [block.array for block in blocks]


def params():
    return pltpu.CompilerParams(vmem_limit_bytes=KERNEL_VMEM)


def cost(us):
    return pl.CostEstimate(flops=0, bytes_accessed=int(us * 3.0e6), transcendentals=0)


def split_rows(value):
    high = value.astype(bf16)
    low = (value - high.astype(f32)).astype(bf16)
    return jnp.concatenate([high, low], 0)


def halves_sum(value):
    rows = value.shape[0] // 2
    return value[:rows] + value[rows:]


def own_member():
    return lax.axis_index("mode")


def base_of(step, slab):
    return (own_member() ^ step) * slab


def columns_of(ids):
    rows = ids.shape[0]
    filled = jnp.concatenate([ids, jnp.broadcast_to(ids[:1], (8 - rows, ids.shape[1]))], 0)
    return filled.T


def one_hot(iota, ids):
    return jnp.where(iota == ids, 1.0, 0.0).astype(bf16)


def transform_tables(mode_dev, members):
    spectral_modes = mode_dev * members
    samples = 2 * spectral_modes
    row = np.arange(samples)
    parity = (row // mode_dev) % 2
    mode = row // (2 * mode_dev) * mode_dev + row % mode_dev
    phases = 2.0 * np.pi / samples * (np.arange(samples)[None, :] * mode[:, None] % samples)
    inverse = np.where(parity[:, None] == 0, np.cos(phases), np.sin(phases))
    weights = np.where((mode == 0) & (parity == 0), 1.0, 2.0) / samples
    return jnp.asarray(inverse, f32), jnp.asarray(inverse * weights[:, None], f32)


def spread_table(table):
    high = table.astype(bf16)
    low = (table - high.astype(f32)).astype(bf16)
    return jnp.concatenate([high, high, low], 1)


def spread_value(value):
    high = value.astype(bf16)
    low = (value - high.astype(f32)).astype(bf16)
    return jnp.concatenate([high, low, high], 0)


def transform_kernel(members, mode_dev, fields, *refs):
    inverse, forward, velocity = refs[:3]
    blocks = refs[3 : 3 + members]
    outs = refs[-(members // 2) :]
    pair = 2 * mode_dev
    rows = blocks[0].shape[0]
    ordered = []
    for table in (inverse, forward):
        starts = [pl.multiple_of(base_of(step, pair), 8) for step in range(members)]
        ordered.append(jnp.concatenate([table[pl.ds(start, pair), :] for start in starts], 0))
    to_points, to_modes = spread_table(ordered[0].T), spread_table(ordered[1])
    for field in range(fields):
        points = []
        for part in range(3):
            low = (field * 3 + part) * pair
            stacked = jnp.concatenate([block[low : low + pair, :] for block in blocks], 0)
            points.append(
                jnp.dot(to_points, spread_value(stacked), preferred_element_type=f32)
            )
        for part in range(3):
            after, last = (part + 1) % 3, (part + 2) % 3
            cross = velocity[after] * points[last] - velocity[last] * points[after]
            back = jnp.dot(to_modes, spread_value(cross), preferred_element_type=f32)
            low = (field * 3 + part) * pair
            for step in range(members):
                at = (step % 2) * rows + low
                outs[step // 2][at : at + pair, :] = back[step * pair : (step + 1) * pair]


def transform(blocks, velocity, inverse, forward, mode_dev, fields):
    members = len(blocks)
    rows, slab = blocks[0].shape
    return pl.pallas_call(
        functools.partial(transform_kernel, members, mode_dev, fields),
        grid=(1,),
        in_specs=[whole_block(x.shape) for x in (inverse, forward, velocity)]
        + specs(blocks),
        out_specs=[whole_block((2 * rows, slab))] * (members // 2),
        out_shape=[jax.ShapeDtypeStruct((2 * rows, slab), f32)] * (members // 2),
        compiler_params=params(),
        cost_estimate=cost(1),
        name="transform",
    )(inverse, forward, velocity, *arrays(blocks))


def pack_kernel(rows, slab, values, *refs):
    outs, sems = refs[:-1], refs[-1]
    copies = []
    for at in range(2 * len(outs)):
        start = pl.multiple_of(base_of(at, slab), 128)
        half = at % 2
        copies.append(
            pltpu.make_async_copy(
                values.at[:, pl.ds(start, slab)],
                outs[at // 2].at[half * rows : (half + 1) * rows, :],
                sems.at[at],
            )
        )
    for copy in copies:
        copy.start()
    for copy in copies:
        copy.wait()


def pack(values, members, slab):
    rows = values.shape[0]
    anywhere = pl.BlockSpec(memory_space=pl.ANY)
    return pl.pallas_call(
        functools.partial(pack_kernel, rows, slab),
        in_specs=[anywhere],
        out_specs=[anywhere] * (members // 2),
        out_shape=[jax.ShapeDtypeStruct((2 * rows, slab), f32)] * (members // 2),
        scratch_shapes=[pltpu.SemaphoreType.DMA((members,))],
        compiler_params=params(),
        cost_estimate=cost(1),
        name="pack",
    )(values)


def lower_halves_kernel(count, *refs):
    blocks, out, sems = refs[:count], refs[-2], refs[-1]
    rows = blocks[0].shape[0] // 2
    copies = [
        pltpu.make_async_copy(
            block.at[rows:, :], out.at[at * rows : (at + 1) * rows, :], sems.at[at]
        )
        for at, block in enumerate(blocks)
    ]
    for copy in copies:
        copy.start()
    for copy in copies:
        copy.wait()


def lower_halves(blocks, after):
    rows, width = blocks[0].shape[0] // 2, blocks[0].shape[1]
    anywhere = pl.BlockSpec(memory_space=pl.ANY)
    return pl.pallas_call(
        functools.partial(lower_halves_kernel, len(blocks)),
        in_specs=[anywhere] * (len(blocks) + len(after)),
        out_specs=anywhere,
        out_shape=jax.ShapeDtypeStruct((len(blocks) * rows, width), f32),
        scratch_shapes=[pltpu.SemaphoreType.DMA((len(blocks),))],
        compiler_params=params(),
        cost_estimate=cost(0.5),
        name="lower_halves",
    )(*blocks, *after)


def interface_ids(interface, counts):
    width = interface.shape[1]
    cap = width // 2
    lists = jnp.broadcast_to(interface[...], (8, width))
    shifted = pltpu.roll(lists, lax.rem(width - counts[0, 0], width), 1)
    return jnp.concatenate([lists[:1, :cap], shifted[:1, :cap]], 1)


def interface_kernel(count, steps, counts, interface, *refs):
    blocks = refs[:count]
    left, right, hot = refs[-3:]
    width = interface.shape[1]
    ids = interface_ids(interface, counts)
    row = 0
    stacked = []
    for at, block in enumerate(blocks):
        size = block.shape[1]
        iota = lax.broadcasted_iota(jnp.int32, (size, width), 0)
        base = 0 if steps is None else base_of(steps[at], size)
        hot[row : row + size, :] = one_hot(iota, ids - base)
        stacked.append(split_rows(block[...]))
        row += size
    values = jnp.concatenate(stacked, 1)
    got = halves_sum(jnp.dot(values, hot[...], preferred_element_type=f32))
    left[...] = got[:, : width // 2]
    right[...] = got[:, width // 2 :]


def interface_values(blocks, steps, counts, interface, us, after=()):
    rows = blocks[0].shape[0]
    total = sum(block.shape[1] for block in blocks)
    cap = interface.shape[1] // 2
    return pl.pallas_call(
        functools.partial(interface_kernel, len(blocks), steps),
        grid=(1,),
        in_specs=[pl.BlockSpec(memory_space=pltpu.SMEM), whole_block(interface.shape)]
        + specs(blocks)
        + [pl.BlockSpec(memory_space=pl.ANY)] * len(after),
        out_specs=[whole_block((rows, cap))] * 2,
        out_shape=[jax.ShapeDtypeStruct((rows, cap), f32)] * 2,
        scratch_shapes=[pltpu.VMEM((total, 2 * cap), bf16)],
        compiler_params=params(),
        cost_estimate=cost(us),
        name="interface_values",
    )(counts, interface, *arrays(blocks), *after)


def live_rows(conn, live, tile_at):
    tile = conn.shape[1]
    element = tile_at * tile + lax.broadcasted_iota(jnp.int32, conn.shape, 1)
    return jnp.where(element < live[0], conn[...], -1)


def fill_gather(hot, conn, blocks, bases, tile):
    row = 0
    for at, block in enumerate(blocks):
        size = block.shape[1]
        iota = lax.broadcasted_iota(jnp.int32, (size, tile), 0)
        for corner in range(6):
            hot[row : row + size, corner * tile : (corner + 1) * tile] = one_hot(
                iota, conn[corner : corner + 1, :] - bases[at]
            )
        row += size


def fill_values(values, blocks):
    column = 0
    for block in blocks:
        size = block.shape[1]
        values[:, column : column + size] = split_rows(block[...])
        column += size


def magnetic_terms_kernel(count, mode_dev, live, conn, stiffness, mass_r, *refs):
    blocks = refs[:count]
    out, done, values, hot, operator = refs[-5:]
    tile = conn.shape[1]
    done[...] = jnp.zeros_like(done)

    @pl.when(pl.program_id(0) == 0)
    def _():
        fill_values(values, blocks)

    bases = [0]
    for block in blocks[:-1]:
        bases.append(bases[-1] + block.shape[1])
    fill_gather(hot, live_rows(conn, live, pl.program_id(0)), blocks, bases, tile)
    lane = lax.broadcasted_iota(jnp.int32, (8, tile), 0)
    squares = (own_member() * mode_dev + lax.rem(lane, mode_dev)).astype(f32) ** 2
    got = halves_sum(jnp.dot(values[...], hot[...], preferred_element_type=f32))
    for a in range(6):
        for b in range(6):
            operator[a * 6 + b] = diffusivity * (
                stiffness[a, b : b + 1, :] + squares * mass_r[a, b : b + 1, :]
            )
    for low in range(0, out.shape[0], 8):
        for a in range(6):
            total = None
            for b in range(6):
                term = operator[a * 6 + b] * got[low : low + 8, b * tile : (b + 1) * tile]
                total = term if total is None else total + term
            out[low : low + 8, a * tile : (a + 1) * tile] = total


def magnetic_terms(blocks, mode_dev, live, conn, stiffness, mass_r, after):
    rows = blocks[0].shape[0]
    elems = conn.shape[1]
    tile = ELEM_TILE
    total = sum(block.shape[1] for block in blocks)
    elem_block = pl.BlockSpec((6, 6, tile), lambda j: (0, 0, j))
    return pl.pallas_call(
        functools.partial(magnetic_terms_kernel, len(blocks), mode_dev),
        grid=(elems // tile,),
        in_specs=[
            pl.BlockSpec(memory_space=pltpu.SMEM),
            pl.BlockSpec((6, tile), lambda j: (0, j)),
            elem_block,
            elem_block,
        ]
        + specs(blocks)
        + [pl.BlockSpec(memory_space=pl.ANY)] * len(after),
        out_specs=[pl.BlockSpec((rows, 6 * tile), lambda j: (0, j)), whole_block((8, 128))],
        out_shape=[
            jax.ShapeDtypeStruct((rows, 6 * elems), f32),
            jax.ShapeDtypeStruct((8, 128), f32),
        ],
        scratch_shapes=[
            pltpu.VMEM((2 * rows, total), bf16),
            pltpu.VMEM((total, 6 * tile), bf16),
            pltpu.VMEM((36, 8, tile), f32),
        ],
        compiler_params=params(),
        cost_estimate=cost(8),
        name="magnetic_terms",
    )(live, conn, stiffness, mass_r, *arrays(blocks), *after)


def gather_kernel(count, steps, adds, live, conn, *refs):
    blocks = refs[:count]
    refs = refs[count:]
    if adds:
        earlier, refs = refs[0], refs[1:]
    out, done, values, hot = refs
    done[...] = jnp.zeros_like(done)
    tile = conn.shape[1]

    @pl.when(pl.program_id(0) == 0)
    def _():
        fill_values(values, blocks)

    bases = [base_of(step, block.shape[1]) for step, block in zip(steps, blocks)]
    fill_gather(hot, live_rows(conn, live, pl.program_id(0)), blocks, bases, tile)
    got = halves_sum(jnp.dot(values[...], hot[...], preferred_element_type=f32))
    out[...] = got + earlier[...] if adds else got


def gathered(blocks, steps, live, conn, earlier, us):
    rows = blocks[0].shape[0]
    elems = conn.shape[1]
    tile = ELEM_TILE
    total = sum(block.shape[1] for block in blocks)
    wide = pl.BlockSpec((rows, 6 * tile), lambda j: (0, j))
    adds = earlier is not None
    return pl.pallas_call(
        functools.partial(gather_kernel, len(blocks), steps, adds),
        grid=(elems // tile,),
        in_specs=[
            pl.BlockSpec(memory_space=pltpu.SMEM),
            pl.BlockSpec((6, tile), lambda j: (0, j)),
        ]
        + specs(blocks)
        + [wide] * adds,
        out_specs=[wide, whole_block((8, 128))],
        out_shape=[
            jax.ShapeDtypeStruct((rows, 6 * elems), f32),
            jax.ShapeDtypeStruct((8, 128), f32),
        ],
        scratch_shapes=[
            pltpu.VMEM((2 * rows, total), bf16),
            pltpu.VMEM((total, 6 * tile), bf16),
        ],
        compiler_params=params(),
        cost_estimate=cost(us),
        name="gathered",
    )(live, conn, *arrays(blocks), *([earlier] * adds))


def fill_scatter(hot, conn_columns, first, tile):
    iota = lax.broadcasted_iota(jnp.int32, (tile, hot.shape[1]), 1)
    for corner in range(6):
        hot[corner * tile : (corner + 1) * tile, :] = one_hot(
            iota, conn_columns[:, corner : corner + 1] - first
        )


def ghost_terms_kernel(
    first, live, conn, coupling, magnetic_part, electric_part, left, right,
    terms, left_sums, right_sums, values, hot, hot_columns, total_sums
):
    step = pl.program_id(0)
    tile = conn.shape[1]
    cap = left.shape[1]

    @pl.when(step == 0)
    def _():
        fill_values(values, (left, right))
        total_sums[...] = jnp.zeros_like(total_sums)

    ids = live_rows(conn, live, step)
    fill_gather(hot, ids, (left, right), (first, first + cap), tile)
    got = electric_part[...] + halves_sum(
        jnp.dot(values[...], hot[...], preferred_element_type=f32)
    )
    rows = got.shape[0]
    for low in range(0, rows, 16):
        for a in range(6):
            at = slice(a * tile, (a + 1) * tile)
            total = -magnetic_part[low : low + 16, at]
            for b in range(6):
                total = total + coupling[a, b : b + 1, :] * got[low : low + 16, b * tile : (b + 1) * tile]
            high = total.astype(bf16)
            terms[low : low + 16, at] = high
            terms[rows + low : rows + low + 16, at] = (total - high.astype(f32)).astype(bf16)
    fill_scatter(hot_columns, columns_of(ids), first, tile)
    total_sums[...] += halves_sum(
        jnp.dot(terms[...], hot_columns[...], preferred_element_type=f32)
    )

    @pl.when(step == pl.num_programs(0) - 1)
    def _():
        left_sums[...] = total_sums[:, :cap]
        right_sums[...] = total_sums[:, cap:]


def ghost_terms(first, live, conn, coupling, magnetic_part, electric_part, left, right):
    rows, cap = left.shape
    elems = conn.shape[1]
    tile = ELEM_TILE
    wide = pl.BlockSpec((rows, 6 * tile), lambda j: (0, j))
    return pl.pallas_call(
        functools.partial(ghost_terms_kernel, first),
        grid=(elems // tile,),
        in_specs=[
            pl.BlockSpec(memory_space=pltpu.SMEM),
            pl.BlockSpec((6, tile), lambda j: (0, j)),
            pl.BlockSpec((6, 6, tile), lambda j: (0, 0, j)),
            wide,
            wide,
            whole_block((rows, cap)),
            whole_block((rows, cap)),
        ],
        out_specs=[
            pl.BlockSpec((2 * rows, 6 * tile), lambda j: (0, j)),
            whole_block((rows, cap)),
            whole_block((rows, cap)),
        ],
        out_shape=[
            jax.ShapeDtypeStruct((2 * rows, 6 * elems), bf16),
            jax.ShapeDtypeStruct((rows, cap), f32),
            jax.ShapeDtypeStruct((rows, cap), f32),
        ],
        scratch_shapes=[
            pltpu.VMEM((2 * rows, 2 * cap), bf16),
            pltpu.VMEM((2 * cap, 6 * tile), bf16),
            pltpu.VMEM((6 * tile, 2 * cap), bf16),
            pltpu.VMEM((rows, 2 * cap), f32),
        ],
        compiler_params=params(),
        cost_estimate=cost(8),
        name="ghost_terms",
    )(live, conn, coupling, magnetic_part, electric_part, left, right)


def own_sums_kernel(live, conn, terms, out, hot):
    @pl.when(pl.program_id(0) == 0)
    def _():
        out[...] = jnp.zeros_like(out)

    columns = columns_of(live_rows(conn, live, pl.program_id(0)))
    fill_scatter(hot, columns, 0, conn.shape[1])
    out[...] += halves_sum(jnp.dot(terms[...], hot[...], preferred_element_type=f32))


def own_sums(live, conn, terms, nodes):
    rows = terms.shape[0] // 2
    tile = ELEM_TILE
    elems = conn.shape[1]
    return pl.pallas_call(
        own_sums_kernel,
        grid=(elems // tile,),
        in_specs=[
            pl.BlockSpec(memory_space=pltpu.SMEM),
            pl.BlockSpec((6, tile), lambda j: (0, j)),
            pl.BlockSpec((2 * rows, 6 * tile), lambda j: (0, j)),
        ],
        out_specs=whole_block((rows, nodes)),
        out_shape=jax.ShapeDtypeStruct((rows, nodes), f32),
        scratch_shapes=[pltpu.VMEM((6 * tile, nodes), bf16)],
        compiler_params=params(),
        cost_estimate=cost(9),
        name="own_sums",
    )(live, conn, terms)


def finish_kernel(counts, interface, magnetic, sums, left, right, inv_mass, out):
    width = interface.shape[1]
    nodes = out.shape[1]
    iota = lax.broadcasted_iota(jnp.int32, (width, nodes), 1)
    hot = one_hot(iota, columns_of(interface_ids(interface, counts))[:, :1])
    values = jnp.concatenate([split_rows(left[...]), split_rows(right[...])], 1)
    extra = halves_sum(jnp.dot(values, hot, preferred_element_type=f32))
    out[...] = magnetic[...] + time_step * inv_mass[...] * (sums[...] + extra)


def finish(counts, interface, magnetic, sums, left, right, inv_mass):
    return pl.pallas_call(
        finish_kernel,
        in_specs=[pl.BlockSpec(memory_space=pltpu.SMEM)]
        + [pl.BlockSpec(memory_space=pltpu.VMEM)] * 6,
        out_shape=jax.ShapeDtypeStruct(magnetic.shape, f32),
        compiler_params=params(),
        cost_estimate=cost(3),
        name="finish",
    )(counts, interface, magnetic, sums, left, right, inv_mass)


def between_chips(blocks):
    members = lax.axis_size("mode")
    order = sorted(range(1, members // 2), key=lambda t: -t)
    got = {
        t: lax.ppermute(blocks[t], "mode", [(k, k ^ (2 * t)) for k in range(members)])
        for t in order
    }
    return [blocks[0]] + [got[t] for t in range(1, members // 2)]


def between_cores(blocks, after):
    members = lax.axis_size("mode")
    return lax.ppermute(lower_halves(blocks, after), "mode", [(k, k ^ 1) for k in range(members)])


def neighbours(to_left, to_right):
    count = lax.axis_size("mesh")
    from_left = lax.ppermute(to_right, "mesh", [(i, i + 1) for i in range(count - 1)])
    from_right = lax.ppermute(to_left, "mesh", [(i + 1, i) for i in range(count - 1)])
    return from_left, from_right


def on_device(
    magnetic, velocity, stiffness, mass_r, coupling, inv_mass, connect, interface, counts, elem_live
):
    fields, vector_parts, mode_dev, node_dev = magnetic.shape
    rows = fields * vector_parts * mode_dev
    cap = interface.shape[1] // 2
    members = lax.axis_size("mode")
    slab = node_dev // members
    values = magnetic.reshape(rows, node_dev)

    packed = pack(values, members, slab)
    kept = between_chips(packed)
    own = Block(values, rows)
    mag_left, mag_right = neighbours(
        *interface_values([own], None, counts, interface, 1, (packed[0],))
    )
    extended = [own, Block(mag_left, rows), Block(mag_right, rows)]
    swapped = between_cores(kept, (mag_left, mag_right))
    arrived = []
    for t, block in enumerate(kept):
        arrived += [Block(block, rows), Block(swapped, rows, t)]
    inverse, forward = transform_tables(mode_dev, members)
    sent = transform(arrived, velocity, inverse, forward, mode_dev, fields)
    kept = between_chips(sent)
    magnetic_part, done = magnetic_terms(
        extended, mode_dev, elem_live, connect, stiffness, mass_r, (sent[0],)
    )
    swapped = between_cores(kept, (done,))
    electric = []
    for t, block in enumerate(kept):
        electric += [Block(block, rows), Block(swapped, rows, t)]
    steps = tuple(range(members))
    ele_left, ele_right = neighbours(*interface_values(electric, steps, counts, interface, 1))
    electric_part, _ = gathered(electric, steps, elem_live, connect, None, 4)
    terms, left_sums, right_sums = ghost_terms(
        node_dev, elem_live, connect, coupling, magnetic_part, electric_part, ele_left, ele_right
    )
    sum_left, sum_right = neighbours(left_sums, right_sums)
    sums = own_sums(elem_live, connect, terms, node_dev)
    out = finish(counts, interface, values, sums, sum_left, sum_right, inv_mass[None, :])
    return out.reshape(magnetic.shape)


def solution(mesh):
    return jax.shard_map(
        on_device,
        mesh=mesh,
        in_specs=(
            P(None, None, "mode", "mesh"),
            P(None, None, ("mesh", "mode")),
            P(None, None, "mesh"),
            P(None, None, "mesh"),
            P(None, None, "mesh"),
            P("mesh"),
            P(None, "mesh"),
            P("mesh", None),
            P("mesh", None),
            P("mesh"),
        ),
        out_specs=P(None, None, "mode", "mesh"),
        check_vma=False,
    )
```

```python
import functools
import math

import jax
import jax.numpy as jnp
import numpy as np
from jax import lax
from jax.experimental import pallas as pl
from jax.experimental.pallas import tpu as pltpu
from jax.sharding import PartitionSpec as P

diffusivity = 1.0
time_step = 0.1
f32 = jnp.float32
bf16 = jnp.bfloat16
KERNEL_VMEM = 20 << 20
ELEM_TILE = 256


def whole_block(shape):
    return pl.BlockSpec(shape, lambda *ids: (0,) * len(shape))


class Block:
    def __init__(self, array, rows, at=0):
        self.array, self.rows, self.at = array, rows, at
        self.shape = (rows, array.shape[1])

    def spec(self):
        at = self.at
        return pl.BlockSpec(self.shape, lambda *ids: (at, 0))


def specs(blocks):
    return [block.spec() for block in blocks]


def arrays(blocks):
    return [block.array for block in blocks]


def params(vmem=KERNEL_VMEM):
    return pltpu.CompilerParams(vmem_limit_bytes=vmem)


def cost(us):
    return pl.CostEstimate(flops=0, bytes_accessed=int(us * 3.0e6), transcendentals=0)


def split_rows(value):
    high = value.astype(bf16)
    low = (value - high.astype(f32)).astype(bf16)
    return jnp.concatenate([high, low], 0)


def halves_sum(value):
    rows = value.shape[0] // 2
    return value[:rows] + value[rows:]


def own_member():
    return lax.axis_index("mode")


def base_of(step, slab):
    return (own_member() ^ step) * slab


def columns_of(ids):
    rows = ids.shape[0]
    filled = jnp.concatenate([ids, jnp.broadcast_to(ids[:1], (8 - rows, ids.shape[1]))], 0)
    return filled.T


def one_hot(iota, ids):
    return jnp.where(iota == ids, 1.0, 0.0).astype(bf16)


def transform_tables(mode_dev, members):
    spectral_modes = mode_dev * members
    samples = 2 * spectral_modes
    row = np.arange(samples)
    parity = (row // mode_dev) % 2
    mode = row // (2 * mode_dev) * mode_dev + row % mode_dev
    phases = 2.0 * np.pi / samples * (np.arange(samples)[None, :] * mode[:, None] % samples)
    inverse = np.where(parity[:, None] == 0, np.cos(phases), np.sin(phases))
    weights = np.where((mode == 0) & (parity == 0), 1.0, 2.0) / samples
    return jnp.asarray(inverse, f32), jnp.asarray(inverse * weights[:, None], f32)


def spread_table(table):
    high = table.astype(bf16)
    low = (table - high.astype(f32)).astype(bf16)
    return jnp.concatenate([high, high, low], 1)


def spread_value(value):
    high = value.astype(bf16)
    low = (value - high.astype(f32)).astype(bf16)
    return jnp.concatenate([high, low, high], 0)


def transform_kernel(members, mode_dev, fields, *refs):
    inverse, forward, velocity = refs[:3]
    blocks = refs[3 : 3 + members]
    outs = refs[-(members // 2) :]
    pair = 2 * mode_dev
    rows = blocks[0].shape[0]
    ordered = []
    for table in (inverse, forward):
        starts = [pl.multiple_of(base_of(step, pair), 8) for step in range(members)]
        ordered.append(jnp.concatenate([table[pl.ds(start, pair), :] for start in starts], 0))
    to_points, to_modes = spread_table(ordered[0].T), spread_table(ordered[1])
    for field in range(fields):
        points = []
        for part in range(3):
            low = (field * 3 + part) * pair
            stacked = jnp.concatenate([block[low : low + pair, :] for block in blocks], 0)
            points.append(
                jnp.dot(to_points, spread_value(stacked), preferred_element_type=f32)
            )
        for part in range(3):
            after, last = (part + 1) % 3, (part + 2) % 3
            cross = velocity[after] * points[last] - velocity[last] * points[after]
            back = jnp.dot(to_modes, spread_value(cross), preferred_element_type=f32)
            low = (field * 3 + part) * pair
            for step in range(members):
                at = (step % 2) * rows + low
                outs[step // 2][at : at + pair, :] = back[step * pair : (step + 1) * pair]


def transform(blocks, velocity, inverse, forward, mode_dev, fields):
    members = len(blocks)
    rows, slab = blocks[0].shape
    return pl.pallas_call(
        functools.partial(transform_kernel, members, mode_dev, fields),
        grid=(1,),
        in_specs=[whole_block(x.shape) for x in (inverse, forward, velocity)]
        + specs(blocks),
        out_specs=[whole_block((2 * rows, slab))] * (members // 2),
        out_shape=[jax.ShapeDtypeStruct((2 * rows, slab), f32)] * (members // 2),
        compiler_params=params(),
        cost_estimate=cost(1),
        name="transform",
    )(inverse, forward, velocity, *arrays(blocks))


def pack_kernel(chips, rows, slab, values, *refs):
    outs, sems = refs[-1 - len(chips) : -1], refs[-1]
    copies = []
    for at in range(2 * len(chips)):
        start = pl.multiple_of(base_of(2 * chips[at // 2] + at % 2, slab), 128)
        half = at % 2
        copies.append(
            pltpu.make_async_copy(
                values.at[:, pl.ds(start, slab)],
                outs[at // 2].at[half * rows : (half + 1) * rows, :],
                sems.at[at],
            )
        )
    for copy in copies:
        copy.start()
    for copy in copies:
        copy.wait()


def pack(values, chips, slab, after):
    rows = values.shape[0]
    anywhere = pl.BlockSpec(memory_space=pl.ANY)
    return pl.pallas_call(
        functools.partial(pack_kernel, chips, rows, slab),
        in_specs=[pl.BlockSpec(memory_space=pltpu.HBM)] + [anywhere] * len(after),
        out_specs=[anywhere] * len(chips),
        out_shape=[jax.ShapeDtypeStruct((2 * rows, slab), f32)] * len(chips),
        scratch_shapes=[pltpu.SemaphoreType.DMA((2 * len(chips),))],
        compiler_params=params(),
        cost_estimate=cost(0.5),
        name="pack",
    )(values, *after)


def relay_kernel(source, *refs):
    copy = pltpu.make_async_copy(source, refs[-2], refs[-1])
    copy.start()
    copy.wait()


def relay(source, after):
    anywhere = pl.BlockSpec(memory_space=pl.ANY)
    return pl.pallas_call(
        relay_kernel,
        in_specs=[anywhere] * (1 + len(after)),
        out_specs=anywhere,
        out_shape=jax.ShapeDtypeStruct(source.shape, f32),
        scratch_shapes=[pltpu.SemaphoreType.DMA],
        compiler_params=params(),
        cost_estimate=cost(0.5),
        name="relay",
    )(source, *after)


def lower_halves_kernel(count, *refs):
    blocks, out, sems = refs[:count], refs[-2], refs[-1]
    rows = blocks[0].shape[0] // 2
    copies = [
        pltpu.make_async_copy(
            block.at[rows:, :], out.at[at * rows : (at + 1) * rows, :], sems.at[at]
        )
        for at, block in enumerate(blocks)
    ]
    for copy in copies:
        copy.start()
    for copy in copies:
        copy.wait()


def lower_halves(blocks, after):
    rows, width = blocks[0].shape[0] // 2, blocks[0].shape[1]
    anywhere = pl.BlockSpec(memory_space=pl.ANY)
    return pl.pallas_call(
        functools.partial(lower_halves_kernel, len(blocks)),
        in_specs=[anywhere] * (len(blocks) + len(after)),
        out_specs=anywhere,
        out_shape=jax.ShapeDtypeStruct((len(blocks) * rows, width), f32),
        scratch_shapes=[pltpu.SemaphoreType.DMA((len(blocks),))],
        compiler_params=params(),
        cost_estimate=cost(0.5),
        name="lower_halves",
    )(*blocks, *after)


def even_partition():
    return lax.rem(lax.axis_index("mesh"), 2) == 0


def interface_ids(interface, counts):
    width = interface.shape[1]
    cap = width // 2
    lists = jnp.broadcast_to(interface[...], (8, width))
    shifted = pltpu.roll(lists, lax.rem(width - counts[0, 0], width), 1)
    left, right = lists[:1, :cap], shifted[:1, :cap]
    even = even_partition()
    return jnp.concatenate([jnp.where(even, right, left), jnp.where(even, left, right)], 1)


def by_partner(ids, first, cap):
    swapped = jnp.where(ids < first + cap, ids + cap, ids - cap)
    return jnp.where((ids >= first) & even_partition(), swapped, ids)


def interface_kernel(count, steps, counts, interface, *refs):
    blocks = refs[:count]
    one, two, hot = refs[-3:]
    width = interface.shape[1]
    ids = interface_ids(interface, counts)
    row = 0
    stacked = []
    for at, block in enumerate(blocks):
        size = block.shape[1]
        iota = lax.broadcasted_iota(jnp.int32, (size, width), 0)
        base = 0 if steps is None else base_of(steps[at], size)
        hot[row : row + size, :] = one_hot(iota, ids - base)
        stacked.append(split_rows(block[...]))
        row += size
    values = jnp.concatenate(stacked, 1)
    got = halves_sum(jnp.dot(values, hot[...], preferred_element_type=f32))
    one[...] = got[:, : width // 2]
    two[...] = got[:, width // 2 :]


def interface_values(blocks, steps, counts, interface, us, after=()):
    rows = blocks[0].shape[0]
    total = sum(block.shape[1] for block in blocks)
    cap = interface.shape[1] // 2
    return pl.pallas_call(
        functools.partial(interface_kernel, len(blocks), steps),
        grid=(1,),
        in_specs=[pl.BlockSpec(memory_space=pltpu.SMEM), whole_block(interface.shape)]
        + specs(blocks)
        + [pl.BlockSpec(memory_space=pl.ANY)] * len(after),
        out_specs=[whole_block((rows, cap))] * 2,
        out_shape=[jax.ShapeDtypeStruct((rows, cap), f32)] * 2,
        scratch_shapes=[pltpu.VMEM((total, 2 * cap), bf16)],
        compiler_params=params(),
        cost_estimate=cost(us),
        name="interface_values",
    )(counts, interface, *arrays(blocks), *after)


def live_rows(conn, live, tile_at):
    tile = conn.shape[1]
    element = tile_at * tile + lax.broadcasted_iota(jnp.int32, conn.shape, 1)
    return jnp.where(element < live[0], conn[...], -1)


def fill_gather(hot, conn, blocks, bases, tile):
    row = 0
    for at, block in enumerate(blocks):
        size = block.shape[1]
        iota = lax.broadcasted_iota(jnp.int32, (size, tile), 0)
        for corner in range(6):
            hot[row : row + size, corner * tile : (corner + 1) * tile] = one_hot(
                iota, conn[corner : corner + 1, :] - bases[at]
            )
        row += size


def fill_values(values, blocks):
    column = 0
    for block in blocks:
        size = block.shape[1]
        values[:, column : column + size] = split_rows(block[...])
        column += size


def magnetic_terms_kernel(count, mode_dev, live, conn, stiffness, mass_r, *refs):
    blocks = refs[:count]
    out, done, values, hot, operator = refs[-5:]
    tile = conn.shape[1]
    done[...] = jnp.zeros_like(done)

    @pl.when(pl.program_id(0) == 0)
    def _():
        fill_values(values, blocks)

    bases = [0]
    for block in blocks[:-1]:
        bases.append(bases[-1] + block.shape[1])
    ids = by_partner(live_rows(conn, live, pl.program_id(0)), bases[1], blocks[1].shape[1])
    fill_gather(hot, ids, blocks, bases, tile)
    lane = lax.broadcasted_iota(jnp.int32, (8, tile), 0)
    squares = (own_member() * mode_dev + lax.rem(lane, mode_dev)).astype(f32) ** 2
    got = halves_sum(jnp.dot(values[...], hot[...], preferred_element_type=f32))
    for a in range(6):
        for b in range(6):
            operator[a * 6 + b] = diffusivity * (
                stiffness[a, b : b + 1, :] + squares * mass_r[a, b : b + 1, :]
            )
    for low in range(0, out.shape[0], 8):
        for a in range(6):
            total = None
            for b in range(6):
                term = operator[a * 6 + b] * got[low : low + 8, b * tile : (b + 1) * tile]
                total = term if total is None else total + term
            out[low : low + 8, a * tile : (a + 1) * tile] = total


def magnetic_terms(blocks, mode_dev, live, conn, stiffness, mass_r, after):
    rows = blocks[0].shape[0]
    elems = conn.shape[1]
    tile = ELEM_TILE
    total = sum(block.shape[1] for block in blocks)
    elem_block = pl.BlockSpec((6, 6, tile), lambda j: (0, 0, j))
    return pl.pallas_call(
        functools.partial(magnetic_terms_kernel, len(blocks), mode_dev),
        grid=(elems // tile,),
        in_specs=[
            pl.BlockSpec(memory_space=pltpu.SMEM),
            pl.BlockSpec((6, tile), lambda j: (0, j)),
            elem_block,
            elem_block,
        ]
        + specs(blocks)
        + [pl.BlockSpec(memory_space=pl.ANY)] * len(after),
        out_specs=[pl.BlockSpec((rows, 6 * tile), lambda j: (0, j)), whole_block((8, 128))],
        out_shape=[
            jax.ShapeDtypeStruct((rows, 6 * elems), f32),
            jax.ShapeDtypeStruct((8, 128), f32),
        ],
        scratch_shapes=[
            pltpu.VMEM((2 * rows, total), bf16),
            pltpu.VMEM((total, 6 * tile), bf16),
            pltpu.VMEM((36, 8, tile), f32),
        ],
        compiler_params=params(),
        cost_estimate=cost(8),
        name="magnetic_terms",
    )(live, conn, stiffness, mass_r, *arrays(blocks), *after)


def gather_kernel(count, steps, adds, live, conn, *refs):
    blocks = refs[:count]
    refs = refs[count:]
    if adds:
        earlier, refs = refs[0], refs[1:]
    out, done, values, hot = refs
    done[...] = jnp.zeros_like(done)
    tile = conn.shape[1]

    @pl.when(pl.program_id(0) == 0)
    def _():
        fill_values(values, blocks)

    bases = [base_of(step, block.shape[1]) for step, block in zip(steps, blocks)]
    fill_gather(hot, live_rows(conn, live, pl.program_id(0)), blocks, bases, tile)
    got = halves_sum(jnp.dot(values[...], hot[...], preferred_element_type=f32))
    out[...] = got + earlier[...] if adds else got


def gathered(blocks, steps, live, conn, earlier, us):
    rows = blocks[0].shape[0]
    elems = conn.shape[1]
    tile = ELEM_TILE
    total = sum(block.shape[1] for block in blocks)
    wide = pl.BlockSpec((rows, 6 * tile), lambda j: (0, j))
    adds = earlier is not None
    return pl.pallas_call(
        functools.partial(gather_kernel, len(blocks), steps, adds),
        grid=(elems // tile,),
        in_specs=[
            pl.BlockSpec(memory_space=pltpu.SMEM),
            pl.BlockSpec((6, tile), lambda j: (0, j)),
        ]
        + specs(blocks)
        + [wide] * adds,
        out_specs=[wide, whole_block((8, 128))],
        out_shape=[
            jax.ShapeDtypeStruct((rows, 6 * elems), f32),
            jax.ShapeDtypeStruct((8, 128), f32),
        ],
        scratch_shapes=[
            pltpu.VMEM((2 * rows, total), bf16),
            pltpu.VMEM((total, 6 * tile), bf16),
        ],
        compiler_params=params(),
        cost_estimate=cost(us),
        name="gathered",
    )(live, conn, *arrays(blocks), *([earlier] * adds))


def fill_scatter(hot, conn_columns, first, tile):
    iota = lax.broadcasted_iota(jnp.int32, (tile, hot.shape[1]), 1)
    for corner in range(6):
        hot[corner * tile : (corner + 1) * tile, :] = one_hot(
            iota, conn_columns[:, corner : corner + 1] - first
        )


def ghost_terms_kernel(
    first, live, conn, coupling, magnetic_part, electric_part, left, right,
    terms, left_sums, right_sums, values, hot, hot_columns, total_sums
):
    step = pl.program_id(0)
    tile = conn.shape[1]
    cap = left.shape[1]

    @pl.when(step == 0)
    def _():
        fill_values(values, (left, right))
        total_sums[...] = jnp.zeros_like(total_sums)

    ids = by_partner(live_rows(conn, live, step), first, cap)
    fill_gather(hot, ids, (left, right), (first, first + cap), tile)
    got = electric_part[...] + halves_sum(
        jnp.dot(values[...], hot[...], preferred_element_type=f32)
    )
    rows = got.shape[0]
    for low in range(0, rows, 16):
        for a in range(6):
            at = slice(a * tile, (a + 1) * tile)
            total = -magnetic_part[low : low + 16, at]
            for b in range(6):
                total = total + coupling[a, b : b + 1, :] * got[low : low + 16, b * tile : (b + 1) * tile]
            high = total.astype(bf16)
            terms[low : low + 16, at] = high
            terms[rows + low : rows + low + 16, at] = (total - high.astype(f32)).astype(bf16)
    fill_scatter(hot_columns, columns_of(ids), first, tile)
    total_sums[...] += halves_sum(
        jnp.dot(terms[...], hot_columns[...], preferred_element_type=f32)
    )

    @pl.when(step == pl.num_programs(0) - 1)
    def _():
        left_sums[...] = total_sums[:, :cap]
        right_sums[...] = total_sums[:, cap:]


def ghost_terms(first, live, conn, coupling, magnetic_part, electric_part, left, right):
    rows, cap = left.shape
    elems = conn.shape[1]
    tile = ELEM_TILE
    wide = pl.BlockSpec((rows, 6 * tile), lambda j: (0, j))
    return pl.pallas_call(
        functools.partial(ghost_terms_kernel, first),
        grid=(elems // tile,),
        in_specs=[
            pl.BlockSpec(memory_space=pltpu.SMEM),
            pl.BlockSpec((6, tile), lambda j: (0, j)),
            pl.BlockSpec((6, 6, tile), lambda j: (0, 0, j)),
            wide,
            wide,
            whole_block((rows, cap)),
            whole_block((rows, cap)),
        ],
        out_specs=[
            pl.BlockSpec((2 * rows, 6 * tile), lambda j: (0, j)),
            whole_block((rows, cap)),
            whole_block((rows, cap)),
        ],
        out_shape=[
            jax.ShapeDtypeStruct((2 * rows, 6 * elems), bf16),
            jax.ShapeDtypeStruct((rows, cap), f32),
            jax.ShapeDtypeStruct((rows, cap), f32),
        ],
        scratch_shapes=[
            pltpu.VMEM((2 * rows, 2 * cap), bf16),
            pltpu.VMEM((2 * cap, 6 * tile), bf16),
            pltpu.VMEM((6 * tile, 2 * cap), bf16),
            pltpu.VMEM((rows, 2 * cap), f32),
        ],
        compiler_params=params(),
        cost_estimate=cost(8),
        name="ghost_terms",
    )(live, conn, coupling, magnetic_part, electric_part, left, right)


def own_sums_kernel(live, conn, terms, out, hot):
    @pl.when(pl.program_id(0) == 0)
    def _():
        out[...] = jnp.zeros_like(out)

    columns = columns_of(live_rows(conn, live, pl.program_id(0)))
    fill_scatter(hot, columns, 0, conn.shape[1])
    out[...] += halves_sum(jnp.dot(terms[...], hot[...], preferred_element_type=f32))


def own_sums(live, conn, terms, nodes):
    rows = terms.shape[0] // 2
    tile = ELEM_TILE
    elems = conn.shape[1]
    return pl.pallas_call(
        own_sums_kernel,
        grid=(elems // tile,),
        in_specs=[
            pl.BlockSpec(memory_space=pltpu.SMEM),
            pl.BlockSpec((6, tile), lambda j: (0, j)),
            pl.BlockSpec((2 * rows, 6 * tile), lambda j: (0, j)),
        ],
        out_specs=whole_block((rows, nodes)),
        out_shape=jax.ShapeDtypeStruct((rows, nodes), f32),
        scratch_shapes=[pltpu.VMEM((6 * tile, nodes), bf16)],
        compiler_params=params(),
        cost_estimate=cost(9),
        name="own_sums",
    )(live, conn, terms)


def interface_hot_kernel(counts, interface, out):
    iota = lax.broadcasted_iota(jnp.int32, out.shape, 1)
    out[...] = one_hot(iota, columns_of(interface_ids(interface, counts))[:, :1])


def interface_hot(counts, interface, nodes):
    return pl.pallas_call(
        interface_hot_kernel,
        in_specs=[
            pl.BlockSpec(memory_space=pltpu.SMEM),
            pl.BlockSpec(memory_space=pltpu.VMEM),
        ],
        out_shape=jax.ShapeDtypeStruct((interface.shape[1], nodes), bf16),
        compiler_params=params(),
        cost_estimate=cost(1),
        name="interface_hot",
    )(counts, interface)


def finish_kernel(hot, magnetic, sums, left, right, inv_mass, out):
    values = jnp.concatenate([split_rows(left[...]), split_rows(right[...])], 1)
    extra = halves_sum(jnp.dot(values, hot[...], preferred_element_type=f32))
    out[...] = magnetic[...] + time_step * inv_mass[...] * (sums[...] + extra)


def finish(hot, magnetic, sums, left, right, inv_mass):
    return pl.pallas_call(
        finish_kernel,
        out_shape=jax.ShapeDtypeStruct(magnetic.shape, f32),
        compiler_params=params(),
        cost_estimate=cost(2),
        name="finish",
    )(hot, magnetic, sums, left, right, inv_mass)


def between_chips(blocks):
    members = lax.axis_size("mode")
    order = sorted(range(1, members // 2), key=lambda t: -t)
    got = {
        t: lax.ppermute(blocks[t], "mode", [(k, k ^ (2 * t)) for k in range(members)])
        for t in order
    }
    return [blocks[0]] + [got[t] for t in range(1, members // 2)]


def between_cores(blocks, after):
    members = lax.axis_size("mode")
    return lax.ppermute(lower_halves(blocks, after), "mode", [(k, k ^ 1) for k in range(members)])


def neighbours(one, two):
    count = lax.axis_size("mesh")
    got = []
    for values, start in ((one, 0), (two, 1)):
        lower = range(start, count - 1, 2)
        pairs = [(i, i + 1) for i in lower] + [(i + 1, i) for i in lower]
        got.append(lax.ppermute(values, "mesh", pairs))
    return got


def on_device(
    magnetic, velocity, stiffness, mass_r, coupling, inv_mass, connect, interface, counts, elem_live
):
    fields, vector_parts, mode_dev, node_dev = magnetic.shape
    rows = fields * vector_parts * mode_dev
    cap = interface.shape[1] // 2
    members = lax.axis_size("mode")
    slab = node_dev // members
    values = magnetic.reshape(rows, node_dev)

    far = pack(values, tuple(range(2, members // 2)), slab, ())
    near = pack(values, (0, 1), slab, (far[0],))
    packed = near + far
    kept = between_chips(packed)
    own = Block(values, rows)
    mag_left, mag_right = neighbours(
        *interface_values([own], None, counts, interface, 1, (packed[0],))
    )
    extended = [own, Block(mag_left, rows), Block(mag_right, rows)]
    hot = interface_hot(counts, interface, node_dev)
    swapped = between_cores(kept, (mag_left, mag_right, hot))
    arrived = []
    for t, block in enumerate(kept):
        arrived += [Block(block, rows), Block(swapped, rows, t)]
    inverse, forward = transform_tables(mode_dev, members)
    sent = list(transform(arrived, velocity, inverse, forward, mode_dev, fields))
    sent[1] = relay(sent[1], (sent[2],))
    kept = between_chips(sent)
    magnetic_part, done = magnetic_terms(
        extended, mode_dev, elem_live, connect, stiffness, mass_r, (sent[1],)
    )
    swapped = between_cores(kept, (done,))
    electric = []
    for t, block in enumerate(kept):
        electric += [Block(block, rows), Block(swapped, rows, t)]
    steps = tuple(range(members))
    ele_left, ele_right = neighbours(*interface_values(electric, steps, counts, interface, 1))
    electric_part, _ = gathered(electric, steps, elem_live, connect, None, 4)
    terms, left_sums, right_sums = ghost_terms(
        node_dev, elem_live, connect, coupling, magnetic_part, electric_part, ele_left, ele_right
    )
    sum_left, sum_right = neighbours(left_sums, right_sums)
    sums = own_sums(elem_live, connect, terms, node_dev)
    out = finish(hot, values, sums, sum_left, sum_right, inv_mass[None, :])
    return out.reshape(magnetic.shape)


def solution(mesh):
    return jax.shard_map(
        on_device,
        mesh=mesh,
        in_specs=(
            P(None, None, "mode", "mesh"),
            P(None, None, ("mesh", "mode")),
            P(None, None, "mesh"),
            P(None, None, "mesh"),
            P(None, None, "mesh"),
            P("mesh"),
            P(None, "mesh"),
            P("mesh", None),
            P("mesh", None),
            P("mesh"),
        ),
        out_specs=P(None, None, "mode", "mesh"),
        check_vma=False,
    )
```

```python
import functools
import math

import jax
import jax.numpy as jnp
import numpy as np
from jax import lax
from jax.experimental import pallas as pl
from jax.experimental.pallas import tpu as pltpu
from jax.sharding import PartitionSpec as P

diffusivity = 1.0
time_step = 0.1
f32 = jnp.float32
bf16 = jnp.bfloat16
KERNEL_VMEM = 20 << 20
ELEM_TILE = 256


def whole_block(shape):
    return pl.BlockSpec(shape, lambda *ids: (0,) * len(shape))


class Block:
    def __init__(self, array, rows, at=0):
        self.array, self.rows, self.at = array, rows, at
        self.shape = (rows, array.shape[1])

    def spec(self):
        at = self.at
        return pl.BlockSpec(self.shape, lambda *ids: (at, 0))


def specs(blocks):
    return [block.spec() for block in blocks]


def arrays(blocks):
    return [block.array for block in blocks]


def operands(blocks):
    given, places = [], []
    for block in blocks:
        found = [array is block.array for array in given]
        if True not in found:
            found.append(True)
            given.append(block.array)
        places.append((found.index(True), block.at * block.rows, block.rows))
    return given, tuple(places)


def views(places, refs):
    return [refs[at].at[low : low + rows, :] for at, low, rows in places]


vmem = pl.BlockSpec(memory_space=pltpu.VMEM)
smem = pl.BlockSpec(memory_space=pltpu.SMEM)
anywhere = pl.BlockSpec(memory_space=pl.ANY)


def params(vmem=KERNEL_VMEM):
    return pltpu.CompilerParams(vmem_limit_bytes=vmem)


def cost(us):
    return pl.CostEstimate(flops=0, bytes_accessed=int(us * 3.0e6), transcendentals=0)


def split_rows(value):
    high = value.astype(bf16)
    low = (value - high.astype(f32)).astype(bf16)
    return jnp.concatenate([high, low], 0)


def halves_sum(value):
    rows = value.shape[0] // 2
    return value[:rows] + value[rows:]


def own_member():
    return lax.axis_index("mode")


def base_of(step, slab):
    return (own_member() ^ step) * slab


def columns_of(ids):
    rows = ids.shape[0]
    filled = jnp.concatenate([ids, jnp.broadcast_to(ids[:1], (8 - rows, ids.shape[1]))], 0)
    return filled.T


def one_hot(iota, ids):
    return jnp.where(iota == ids, 1.0, 0.0).astype(bf16)


def transform_tables(mode_dev, members):
    spectral_modes = mode_dev * members
    samples = 2 * spectral_modes
    row = np.arange(samples)
    parity = (row // mode_dev) % 2
    mode = row // (2 * mode_dev) * mode_dev + row % mode_dev
    phases = 2.0 * np.pi / samples * (np.arange(samples)[None, :] * mode[:, None] % samples)
    inverse = np.where(parity[:, None] == 0, np.cos(phases), np.sin(phases))
    weights = np.where((mode == 0) & (parity == 0), 1.0, 2.0) / samples
    return jnp.asarray(inverse, f32), jnp.asarray(inverse * weights[:, None], f32)


def spread_table(table):
    high = table.astype(bf16)
    low = (table - high.astype(f32)).astype(bf16)
    return jnp.concatenate([high, high, low], 1)


def spread_value(value):
    high = value.astype(bf16)
    low = (value - high.astype(f32)).astype(bf16)
    return jnp.concatenate([high, low, high], 0)


def transform_kernel(members, mode_dev, fields, *refs):
    inverse, forward, velocity = refs[:3]
    blocks = refs[3 : 3 + members]
    outs = refs[-(members // 2) :]
    pair = 2 * mode_dev
    rows = blocks[0].shape[0]
    ordered = []
    for table in (inverse, forward):
        starts = [pl.multiple_of(base_of(step, pair), 8) for step in range(members)]
        ordered.append(jnp.concatenate([table[pl.ds(start, pair), :] for start in starts], 0))
    to_points, to_modes = spread_table(ordered[0].T), spread_table(ordered[1])
    for field in range(fields):
        points = []
        for part in range(3):
            low = (field * 3 + part) * pair
            stacked = jnp.concatenate([block[low : low + pair, :] for block in blocks], 0)
            points.append(
                jnp.dot(to_points, spread_value(stacked), preferred_element_type=f32)
            )
        for part in range(3):
            after, last = (part + 1) % 3, (part + 2) % 3
            cross = velocity[after] * points[last] - velocity[last] * points[after]
            back = jnp.dot(to_modes, spread_value(cross), preferred_element_type=f32)
            low = (field * 3 + part) * pair
            for step in range(members):
                at = (step % 2) * rows + low
                outs[step // 2][at : at + pair, :] = back[step * pair : (step + 1) * pair]


def transform(blocks, velocity, inverse, forward, mode_dev, fields):
    members = len(blocks)
    rows, slab = blocks[0].shape
    return pl.pallas_call(
        functools.partial(transform_kernel, members, mode_dev, fields),
        grid=(1,),
        in_specs=[whole_block(x.shape) for x in (inverse, forward, velocity)]
        + specs(blocks),
        out_specs=[whole_block((2 * rows, slab))] * (members // 2),
        out_shape=[jax.ShapeDtypeStruct((2 * rows, slab), f32)] * (members // 2),
        compiler_params=params(),
        cost_estimate=cost(1),
        name="transform",
    )(inverse, forward, velocity, *arrays(blocks))


def pack_kernel(chips, rows, slab, values, *refs):
    outs, sems = refs[-1 - len(chips) : -1], refs[-1]
    copies = []
    for at in range(2 * len(chips)):
        start = pl.multiple_of(base_of(2 * chips[at // 2] + at % 2, slab), 128)
        half = at % 2
        copies.append(
            pltpu.make_async_copy(
                values.at[:, pl.ds(start, slab)],
                outs[at // 2].at[half * rows : (half + 1) * rows, :],
                sems.at[at],
            )
        )
    for copy in copies:
        copy.start()
    for copy in copies:
        copy.wait()


def pack(values, chips, slab, after):
    rows = values.shape[0]
    anywhere = pl.BlockSpec(memory_space=pl.ANY)
    return pl.pallas_call(
        functools.partial(pack_kernel, chips, rows, slab),
        in_specs=[pl.BlockSpec(memory_space=pltpu.HBM)] + [anywhere] * len(after),
        out_specs=[anywhere] * len(chips),
        out_shape=[jax.ShapeDtypeStruct((2 * rows, slab), f32)] * len(chips),
        scratch_shapes=[pltpu.SemaphoreType.DMA((2 * len(chips),))],
        compiler_params=params(),
        cost_estimate=cost(0.5),
        name="pack",
    )(values, *after)


def relay_kernel(source, *refs):
    copy = pltpu.make_async_copy(source, refs[-2], refs[-1])
    copy.start()
    copy.wait()


def relay(source, after):
    anywhere = pl.BlockSpec(memory_space=pl.ANY)
    return pl.pallas_call(
        relay_kernel,
        in_specs=[anywhere] * (1 + len(after)),
        out_specs=anywhere,
        out_shape=jax.ShapeDtypeStruct(source.shape, f32),
        scratch_shapes=[pltpu.SemaphoreType.DMA],
        compiler_params=params(),
        cost_estimate=cost(0.5),
        name="relay",
    )(source, *after)


def lower_halves_kernel(count, *refs):
    blocks, out, sems = refs[:count], refs[-2], refs[-1]
    rows = blocks[0].shape[0] // 2
    copies = [
        pltpu.make_async_copy(
            block.at[rows:, :], out.at[at * rows : (at + 1) * rows, :], sems.at[at]
        )
        for at, block in enumerate(blocks)
    ]
    for copy in copies:
        copy.start()
    for copy in copies:
        copy.wait()


def lower_halves(blocks, after):
    rows, width = blocks[0].shape[0] // 2, blocks[0].shape[1]
    anywhere = pl.BlockSpec(memory_space=pl.ANY)
    return pl.pallas_call(
        functools.partial(lower_halves_kernel, len(blocks)),
        in_specs=[anywhere] * (len(blocks) + len(after)),
        out_specs=anywhere,
        out_shape=jax.ShapeDtypeStruct((len(blocks) * rows, width), f32),
        scratch_shapes=[pltpu.SemaphoreType.DMA((len(blocks),))],
        compiler_params=params(),
        cost_estimate=cost(0.01),
        name="lower_halves",
    )(*blocks, *after)


def even_partition():
    return lax.rem(lax.axis_index("mesh"), 2) == 0


def interface_ids(interface, counts):
    width = interface.shape[1]
    cap = width // 2
    lists = jnp.broadcast_to(interface[...], (8, width))
    shifted = pltpu.roll(lists, lax.rem(width - counts[0, 0], width), 1)
    left, right = lists[:1, :cap], shifted[:1, :cap]
    even = even_partition()
    return jnp.concatenate([jnp.where(even, right, left), jnp.where(even, left, right)], 1)


def by_partner(ids, first, cap):
    swapped = jnp.where(ids < first + cap, ids + cap, ids - cap)
    return jnp.where((ids >= first) & even_partition(), swapped, ids)


def interface_kernel(places, steps, counts, interface, *refs):
    one, two, hot = refs[-3:]
    width = interface.shape[1]
    ids = interface_ids(interface, counts)
    row = 0
    stacked = []
    for view, step in zip(views(places, refs), steps):
        block = view[...]
        size = block.shape[1]
        iota = lax.broadcasted_iota(jnp.int32, (size, width), 0)
        base = 0 if step is None else base_of(step, size)
        hot[row : row + size, :] = one_hot(iota, ids - base)
        stacked.append(split_rows(block))
        row += size
    values = jnp.concatenate(stacked, 1)
    got = halves_sum(jnp.dot(values, hot[...], preferred_element_type=f32))
    one[...] = got[:, : width // 2]
    two[...] = got[:, width // 2 :]


def interface_values(blocks, steps, counts, interface, us, after=()):
    rows = blocks[0].shape[0]
    total = sum(block.shape[1] for block in blocks)
    cap = interface.shape[1] // 2
    given, places = operands(blocks)
    return pl.pallas_call(
        functools.partial(interface_kernel, places, steps),
        in_specs=[pl.BlockSpec(memory_space=pltpu.SMEM)]
        + [vmem] * (1 + len(given))
        + [pl.BlockSpec(memory_space=pl.ANY)] * len(after),
        out_shape=[jax.ShapeDtypeStruct((rows, cap), f32)] * 2,
        scratch_shapes=[pltpu.VMEM((total, 2 * cap), bf16)],
        compiler_params=params(),
        cost_estimate=cost(us),
        name="interface_values",
    )(counts, interface, *given, *after)


def tile_ids(conn, live, at, tile):
    ids = conn[:, at * tile : (at + 1) * tile]
    element = at * tile + lax.broadcasted_iota(jnp.int32, ids.shape, 1)
    return jnp.where(element < live[0], ids, -1)


def fill_gather(hot, conn, blocks, bases, tile):
    row = 0
    for at, block in enumerate(blocks):
        size = block.shape[1]
        iota = lax.broadcasted_iota(jnp.int32, (size, tile), 0)
        for corner in range(6):
            hot[row : row + size, corner * tile : (corner + 1) * tile] = one_hot(
                iota, conn[corner : corner + 1, :] - bases[at]
            )
        row += size


def fill_values(values, blocks):
    column = 0
    for block in blocks:
        size = block.shape[1]
        values[:, column : column + size] = split_rows(block[...])
        column += size


def magnetic_terms_kernel(places, mode_dev, live, conn, stiffness, mass_r, *refs):
    blocks = views(places, refs)
    out, done, values, hots, operator = refs[-5:]
    tile = operator.shape[2]
    done[...] = jnp.zeros_like(done)
    fill_values(values, blocks)
    bases = [0]
    for block in blocks[:-1]:
        bases.append(bases[-1] + block.shape[1])
    lane = lax.broadcasted_iota(jnp.int32, (8, tile), 0)
    squares = (own_member() * mode_dev + lax.rem(lane, mode_dev)).astype(f32) ** 2
    for step in range(out.shape[0]):
        hot = hots.at[step % 2]
        ids = by_partner(tile_ids(conn, live, step, tile), bases[1], blocks[1].shape[1])
        fill_gather(hot, ids, blocks, bases, tile)
        got = halves_sum(jnp.dot(values[...], hot[...], preferred_element_type=f32))
        at = slice(step * tile, (step + 1) * tile)
        for a in range(6):
            for b in range(6):
                operator[a * 6 + b] = diffusivity * (
                    stiffness[a, b : b + 1, at] + squares * mass_r[a, b : b + 1, at]
                )
        for low in range(0, out.shape[1], 8):
            for a in range(6):
                total = None
                for b in range(6):
                    term = operator[a * 6 + b] * got[low : low + 8, b * tile : (b + 1) * tile]
                    total = term if total is None else total + term
                out[step, low : low + 8, a * tile : (a + 1) * tile] = total


def magnetic_terms(blocks, mode_dev, live, conn, stiffness, mass_r, after):
    rows = blocks[0].shape[0]
    elems = conn.shape[1]
    tile = ELEM_TILE
    total = sum(block.shape[1] for block in blocks)
    given, places = operands(blocks)
    return pl.pallas_call(
        functools.partial(magnetic_terms_kernel, places, mode_dev),
        in_specs=[smem] + [vmem] * (3 + len(given)) + [anywhere] * len(after),
        out_shape=[
            jax.ShapeDtypeStruct((elems // tile, rows, 6 * tile), f32),
            jax.ShapeDtypeStruct((8, 128), f32),
        ],
        scratch_shapes=[
            pltpu.VMEM((2 * rows, total), bf16),
            pltpu.VMEM((2, total, 6 * tile), bf16),
            pltpu.VMEM((36, 8, tile), f32),
        ],
        compiler_params=params(28 << 20),
        cost_estimate=cost(30),
        name="magnetic_terms",
    )(live, conn, stiffness, mass_r, *given, *after)


def gather_kernel(places, steps, live, conn, *refs):
    blocks = views(places, refs)
    out, values, hots = refs[-3:]
    tile = out.shape[2] // 6
    fill_values(values, blocks)
    bases = [base_of(step, block.shape[1]) for step, block in zip(steps, blocks)]
    for step in range(out.shape[0]):
        hot = hots.at[step % 2]
        fill_gather(hot, tile_ids(conn, live, step, tile), blocks, bases, tile)
        out[step] = halves_sum(jnp.dot(values[...], hot[...], preferred_element_type=f32))


def gathered(blocks, steps, live, conn):
    rows = blocks[0].shape[0]
    elems = conn.shape[1]
    tile = ELEM_TILE
    total = sum(block.shape[1] for block in blocks)
    given, places = operands(blocks)
    return pl.pallas_call(
        functools.partial(gather_kernel, places, steps),
        in_specs=[smem] + [vmem] * (1 + len(given)),
        out_shape=jax.ShapeDtypeStruct((elems // tile, rows, 6 * tile), f32),
        scratch_shapes=[
            pltpu.VMEM((2 * rows, total), bf16),
            pltpu.VMEM((2, total, 6 * tile), bf16),
        ],
        compiler_params=params(28 << 20),
        cost_estimate=cost(5),
        name="gathered",
    )(live, conn, *given)


def fill_scatter(hot, conn_columns, first, tile):
    iota = lax.broadcasted_iota(jnp.int32, (tile, hot.shape[1]), 1)
    for corner in range(6):
        hot[corner * tile : (corner + 1) * tile, :] = one_hot(
            iota, conn_columns[:, corner : corner + 1] - first
        )


def ghost_terms_kernel(
    first, live, conn, coupling, magnetic_part, electric_part, left, right,
    terms, left_sums, right_sums, values, hots, hots_columns
):
    tile = terms.shape[2] // 6
    rows, cap = left.shape
    fill_values(values, (left, right))
    sums = None
    for step in range(terms.shape[0]):
        hot, hot_columns = hots.at[step % 2], hots_columns.at[step % 2]
        ids = by_partner(tile_ids(conn, live, step, tile), first, cap)
        fill_gather(hot, ids, (left, right), (first, first + cap), tile)
        fill_scatter(hot_columns, columns_of(ids), first, tile)
        got = electric_part[step] + halves_sum(
            jnp.dot(values[...], hot[...], preferred_element_type=f32)
        )
        across = slice(step * tile, (step + 1) * tile)
        for low in range(0, rows, 16):
            for a in range(6):
                at = slice(a * tile, (a + 1) * tile)
                total = -magnetic_part[step, low : low + 16, at]
                for b in range(6):
                    total = total + coupling[a, b : b + 1, across] * got[low : low + 16, b * tile : (b + 1) * tile]
                high = total.astype(bf16)
                terms[step, low : low + 16, at] = high
                terms[step, rows + low : rows + low + 16, at] = (total - high.astype(f32)).astype(bf16)
        part = halves_sum(jnp.dot(terms[step], hot_columns[...], preferred_element_type=f32))
        if step == 0:
            left_sums[...] = part[:, :cap]
            right_sums[...] = part[:, cap:]
        else:
            left_sums[...] += part[:, :cap]
            right_sums[...] += part[:, cap:]


def ghost_terms(first, live, conn, coupling, magnetic_part, electric_part, left, right):
    rows, cap = left.shape
    steps, _, wide = electric_part.shape
    return pl.pallas_call(
        functools.partial(ghost_terms_kernel, first),
        in_specs=[smem] + [vmem] * 6,
        out_shape=[
            jax.ShapeDtypeStruct((steps, 2 * rows, wide), bf16),
            jax.ShapeDtypeStruct((rows, cap), f32),
            jax.ShapeDtypeStruct((rows, cap), f32),
        ],
        scratch_shapes=[
            pltpu.VMEM((2 * rows, 2 * cap), bf16),
            pltpu.VMEM((2, 2 * cap, wide), bf16),
            pltpu.VMEM((2, wide, 2 * cap), bf16),
        ],
        compiler_params=params(),
        cost_estimate=cost(8),
        name="ghost_terms",
    )(live, conn, coupling, magnetic_part, electric_part, left, right)


def own_sums_kernel(live, conn, terms, out, hots):
    tile = terms.shape[2] // 6
    for step in range(terms.shape[0]):
        hot = hots.at[step % 2]
        fill_scatter(hot, columns_of(tile_ids(conn, live, step, tile)), 0, tile)
        part = halves_sum(jnp.dot(terms[step], hot[...], preferred_element_type=f32))
        if step == 0:
            out[...] = part
        else:
            out[...] += part


def own_sums(live, conn, terms, nodes):
    rows, wide = terms.shape[1] // 2, terms.shape[2]
    return pl.pallas_call(
        own_sums_kernel,
        in_specs=[smem, vmem, vmem],
        out_shape=jax.ShapeDtypeStruct((rows, nodes), f32),
        scratch_shapes=[pltpu.VMEM((2, wide, nodes), bf16)],
        compiler_params=params(),
        cost_estimate=cost(9),
        name="own_sums",
    )(live, conn, terms)


def interface_hot_kernel(counts, interface, out):
    iota = lax.broadcasted_iota(jnp.int32, out.shape, 1)
    out[...] = one_hot(iota, columns_of(interface_ids(interface, counts))[:, :1])


def interface_hot(counts, interface, nodes):
    return pl.pallas_call(
        interface_hot_kernel,
        in_specs=[
            pl.BlockSpec(memory_space=pltpu.SMEM),
            pl.BlockSpec(memory_space=pltpu.VMEM),
        ],
        out_shape=jax.ShapeDtypeStruct((interface.shape[1], nodes), bf16),
        compiler_params=params(),
        cost_estimate=cost(1),
        name="interface_hot",
    )(counts, interface)


def finish_kernel(hot, magnetic, sums, left, right, inv_mass, out):
    values = jnp.concatenate([split_rows(left[...]), split_rows(right[...])], 1)
    extra = halves_sum(jnp.dot(values, hot[...], preferred_element_type=f32))
    out[...] = magnetic[...] + time_step * inv_mass[...] * (sums[...] + extra)


def finish(hot, magnetic, sums, left, right, inv_mass):
    return pl.pallas_call(
        finish_kernel,
        out_shape=jax.ShapeDtypeStruct(magnetic.shape, f32),
        compiler_params=params(),
        cost_estimate=cost(2),
        name="finish",
    )(hot, magnetic, sums, left, right, inv_mass)


def between_chips(blocks):
    members = lax.axis_size("mode")
    order = sorted(range(1, members // 2), key=lambda t: -t)
    got = {
        t: lax.ppermute(blocks[t], "mode", [(k, k ^ (2 * t)) for k in range(members)])
        for t in order
    }
    return [blocks[0]] + [got[t] for t in range(1, members // 2)]


def between_cores(blocks, after):
    members = lax.axis_size("mode")
    return lax.ppermute(lower_halves(blocks, after), "mode", [(k, k ^ 1) for k in range(members)])


def neighbours(one, two):
    count = lax.axis_size("mesh")
    got = []
    for values, start in ((one, 0), (two, 1)):
        lower = range(start, count - 1, 2)
        pairs = [(i, i + 1) for i in lower] + [(i + 1, i) for i in lower]
        got.append(lax.ppermute(values, "mesh", pairs))
    return got


def on_device(
    magnetic, velocity, stiffness, mass_r, coupling, inv_mass, connect, interface, counts, elem_live
):
    fields, vector_parts, mode_dev, node_dev = magnetic.shape
    rows = fields * vector_parts * mode_dev
    cap = interface.shape[1] // 2
    members = lax.axis_size("mode")
    slab = node_dev // members
    values = magnetic.reshape(rows, node_dev)

    far = pack(values, tuple(range(2, members // 2)), slab, ())
    near = pack(values, (0, 1), slab, (far[0],))
    packed = near + far
    kept = between_chips(packed)
    own = Block(values, rows)
    mag_left, mag_right = neighbours(
        *interface_values([own], (None,), counts, interface, 1, (packed[0],))
    )
    extended = [own, Block(mag_left, rows), Block(mag_right, rows)]
    hot = interface_hot(counts, interface, node_dev)
    swapped = between_cores(kept, (mag_left, mag_right, hot))
    arrived = []
    for t, block in enumerate(kept):
        arrived += [Block(block, rows), Block(swapped, rows, t)]
    inverse, forward = transform_tables(mode_dev, members)
    sent = list(transform(arrived, velocity, inverse, forward, mode_dev, fields))
    sent[1] = relay(sent[1], (sent[2],))
    kept = between_chips(sent)
    magnetic_part, done = magnetic_terms(
        extended, mode_dev, elem_live, connect, stiffness, mass_r, (sent[1],)
    )
    steps = tuple(range(members))
    electric = []
    swapped = between_cores(kept[:2], (done,))
    for t, block in enumerate(kept[:2]):
        electric += [Block(block, rows), Block(swapped, rows, t)]
    swapped = between_cores(kept[2:], ())
    for t, block in enumerate(kept[2:]):
        electric += [Block(block, rows), Block(swapped, rows, t)]
    ele_left, ele_right = neighbours(*interface_values(electric, steps, counts, interface, 1))
    electric_part = gathered(electric, steps, elem_live, connect)
    terms, left_sums, right_sums = ghost_terms(
        node_dev, elem_live, connect, coupling, magnetic_part, electric_part, ele_left, ele_right
    )
    sum_left, sum_right = neighbours(left_sums, right_sums)
    sums = own_sums(elem_live, connect, terms, node_dev)
    out = finish(hot, values, sums, sum_left, sum_right, inv_mass[None, :])
    return out.reshape(magnetic.shape)


def solution(mesh):
    return jax.shard_map(
        on_device,
        mesh=mesh,
        in_specs=(
            P(None, None, "mode", "mesh"),
            P(None, None, ("mesh", "mode")),
            P(None, None, "mesh"),
            P(None, None, "mesh"),
            P(None, None, "mesh"),
            P("mesh"),
            P(None, "mesh"),
            P("mesh", None),
            P("mesh", None),
            P("mesh"),
        ),
        out_specs=P(None, None, "mode", "mesh"),
        check_vma=False,
    )
```

```python
import functools
import math

import jax
import jax.numpy as jnp
import numpy as np
from jax import lax
from jax.experimental import pallas as pl
from jax.experimental.pallas import tpu as pltpu
from jax.sharding import PartitionSpec as P

diffusivity = 1.0
time_step = 0.1
f32 = jnp.float32
bf16 = jnp.bfloat16
KERNEL_VMEM = 20 << 20
ELEM_TILE = 256


def whole_block(shape):
    return pl.BlockSpec(shape, lambda *ids: (0,) * len(shape))


class Block:
    def __init__(self, array, rows, at=0):
        self.array, self.rows, self.at = array, rows, at
        self.shape = (rows, array.shape[1])

    def spec(self):
        at = self.at
        return pl.BlockSpec(self.shape, lambda *ids: (at, 0))


def specs(blocks):
    return [block.spec() for block in blocks]


def arrays(blocks):
    return [block.array for block in blocks]


def operands(blocks):
    given, places = [], []
    for block in blocks:
        found = [array is block.array for array in given]
        if True not in found:
            found.append(True)
            given.append(block.array)
        places.append((found.index(True), block.at * block.rows, block.rows))
    return given, tuple(places)


def views(places, refs):
    return [refs[at].at[low : low + rows, :] for at, low, rows in places]


vmem = pl.BlockSpec(memory_space=pltpu.VMEM)
smem = pl.BlockSpec(memory_space=pltpu.SMEM)
anywhere = pl.BlockSpec(memory_space=pl.ANY)


def params(vmem=KERNEL_VMEM):
    return pltpu.CompilerParams(vmem_limit_bytes=vmem)


def cost(us):
    return pl.CostEstimate(flops=0, bytes_accessed=int(us * 3.0e6), transcendentals=0)


def split_rows(value):
    high = value.astype(bf16)
    low = (value - high.astype(f32)).astype(bf16)
    return jnp.concatenate([high, low], 0)


def halves_sum(value):
    rows = value.shape[0] // 2
    return value[:rows] + value[rows:]


def own_member():
    return lax.axis_index("mode")


def base_of(step, slab):
    return (own_member() ^ step) * slab


def columns_of(ids):
    rows = ids.shape[0]
    filled = jnp.concatenate([ids, jnp.broadcast_to(ids[:1], (8 - rows, ids.shape[1]))], 0)
    return filled.T


def one_hot(iota, ids):
    return jnp.where(iota == ids, 1.0, 0.0).astype(bf16)


def transform_tables(mode_dev, members):
    spectral_modes = mode_dev * members
    samples = 2 * spectral_modes
    row = np.arange(samples)
    parity = (row // mode_dev) % 2
    mode = row // (2 * mode_dev) * mode_dev + row % mode_dev
    phases = 2.0 * np.pi / samples * (np.arange(samples)[None, :] * mode[:, None] % samples)
    inverse = np.where(parity[:, None] == 0, np.cos(phases), np.sin(phases))
    weights = np.where((mode == 0) & (parity == 0), 1.0, 2.0) / samples
    return jnp.asarray(inverse, f32), jnp.asarray(inverse * weights[:, None], f32)


def spread_table(table):
    high = table.astype(bf16)
    low = (table - high.astype(f32)).astype(bf16)
    return jnp.concatenate([high, high, low], 1)


def spread_value(value):
    high = value.astype(bf16)
    low = (value - high.astype(f32)).astype(bf16)
    return jnp.concatenate([high, low, high], 0)


def transform_kernel(members, mode_dev, fields, *refs):
    inverse, forward, velocity = refs[:3]
    blocks = refs[3 : 3 + members]
    outs = refs[-(members // 2) :]
    pair = 2 * mode_dev
    rows = blocks[0].shape[0]
    ordered = []
    for table in (inverse, forward):
        starts = [pl.multiple_of(base_of(step, pair), 8) for step in range(members)]
        ordered.append(jnp.concatenate([table[pl.ds(start, pair), :] for start in starts], 0))
    to_points, to_modes = spread_table(ordered[0].T), spread_table(ordered[1])
    for field in range(fields):
        points = []
        for part in range(3):
            low = (field * 3 + part) * pair
            stacked = jnp.concatenate([block[low : low + pair, :] for block in blocks], 0)
            points.append(
                jnp.dot(to_points, spread_value(stacked), preferred_element_type=f32)
            )
        for part in range(3):
            after, last = (part + 1) % 3, (part + 2) % 3
            cross = velocity[after] * points[last] - velocity[last] * points[after]
            back = jnp.dot(to_modes, spread_value(cross), preferred_element_type=f32)
            low = (field * 3 + part) * pair
            for step in range(members):
                at = (step % 2) * rows + low
                outs[step // 2][at : at + pair, :] = back[step * pair : (step + 1) * pair]


def transform(blocks, velocity, inverse, forward, mode_dev, fields):
    members = len(blocks)
    rows, slab = blocks[0].shape
    return pl.pallas_call(
        functools.partial(transform_kernel, members, mode_dev, fields),
        grid=(1,),
        in_specs=[whole_block(x.shape) for x in (inverse, forward, velocity)]
        + specs(blocks),
        out_specs=[whole_block((2 * rows, slab))] * (members // 2),
        out_shape=[jax.ShapeDtypeStruct((2 * rows, slab), f32)] * (members // 2),
        compiler_params=params(),
        cost_estimate=cost(1),
        name="transform",
    )(inverse, forward, velocity, *arrays(blocks))


def pack_kernel(chips, rows, slab, values, *refs):
    outs, sems = refs[-1 - len(chips) : -1], refs[-1]
    copies = []
    for at in range(2 * len(chips)):
        start = pl.multiple_of(base_of(2 * chips[at // 2] + at % 2, slab), 128)
        half = at % 2
        copies.append(
            pltpu.make_async_copy(
                values.at[:, pl.ds(start, slab)],
                outs[at // 2].at[half * rows : (half + 1) * rows, :],
                sems.at[at],
            )
        )
    for copy in copies:
        copy.start()
    for copy in copies:
        copy.wait()


def pack(values, chips, slab, after):
    rows = values.shape[0]
    anywhere = pl.BlockSpec(memory_space=pl.ANY)
    return pl.pallas_call(
        functools.partial(pack_kernel, chips, rows, slab),
        in_specs=[pl.BlockSpec(memory_space=pltpu.HBM)] + [anywhere] * len(after),
        out_specs=[anywhere] * len(chips),
        out_shape=[jax.ShapeDtypeStruct((2 * rows, slab), f32)] * len(chips),
        scratch_shapes=[pltpu.SemaphoreType.DMA((2 * len(chips),))],
        compiler_params=params(),
        cost_estimate=cost(0.5),
        name="pack",
    )(values, *after)


def relay_kernel(source, *refs):
    copy = pltpu.make_async_copy(source, refs[-2], refs[-1])
    copy.start()
    copy.wait()


def relay(source, after):
    anywhere = pl.BlockSpec(memory_space=pl.ANY)
    return pl.pallas_call(
        relay_kernel,
        in_specs=[anywhere] * (1 + len(after)),
        out_specs=anywhere,
        out_shape=jax.ShapeDtypeStruct(source.shape, f32),
        scratch_shapes=[pltpu.SemaphoreType.DMA],
        compiler_params=params(),
        cost_estimate=cost(0.5),
        name="relay",
    )(source, *after)


def lower_halves_kernel(count, *refs):
    blocks, out, sems = refs[:count], refs[-2], refs[-1]
    rows = blocks[0].shape[0] // 2
    copies = [
        pltpu.make_async_copy(
            block.at[rows:, :], out.at[at * rows : (at + 1) * rows, :], sems.at[at]
        )
        for at, block in enumerate(blocks)
    ]
    for copy in copies:
        copy.start()
    for copy in copies:
        copy.wait()


def lower_halves(blocks, after):
    rows, width = blocks[0].shape[0] // 2, blocks[0].shape[1]
    anywhere = pl.BlockSpec(memory_space=pl.ANY)
    return pl.pallas_call(
        functools.partial(lower_halves_kernel, len(blocks)),
        in_specs=[anywhere] * (len(blocks) + len(after)),
        out_specs=anywhere,
        out_shape=jax.ShapeDtypeStruct((len(blocks) * rows, width), f32),
        scratch_shapes=[pltpu.SemaphoreType.DMA((len(blocks),))],
        compiler_params=params(),
        cost_estimate=cost(0.01),
        name="lower_halves",
    )(*blocks, *after)


def even_partition():
    return lax.rem(lax.axis_index("mesh"), 2) == 0


def interface_ids(interface, counts):
    width = interface.shape[1]
    cap = width // 2
    lists = jnp.broadcast_to(interface[...], (8, width))
    shifted = pltpu.roll(lists, lax.rem(width - counts[0, 0], width), 1)
    left, right = lists[:1, :cap], shifted[:1, :cap]
    even = even_partition()
    return jnp.concatenate([jnp.where(even, right, left), jnp.where(even, left, right)], 1)


def by_partner(ids, first, cap):
    swapped = jnp.where(ids < first + cap, ids + cap, ids - cap)
    return jnp.where((ids >= first) & even_partition(), swapped, ids)


def member_hot(out, ids, steps, slab):
    for at, step in enumerate(steps):
        iota = lax.broadcasted_iota(jnp.int32, (slab, ids.shape[1]), 0)
        base = 0 if step is None else base_of(step, slab)
        out[at * slab : (at + 1) * slab, :] = one_hot(iota, ids - base)


def interface_kernel(places, steps, counts, interface, *refs):
    one, two, hot = refs[-3:]
    blocks = views(places, refs)
    member_hot(hot, interface_ids(interface, counts), steps, blocks[0].shape[1])
    picked_values(blocks, hot, one, two)


def picked_values(blocks, hot, one, two):
    cap = one.shape[1]
    values = jnp.concatenate([split_rows(block[...]) for block in blocks], 1)
    got = halves_sum(jnp.dot(values, hot[...], preferred_element_type=f32))
    one[...] = got[:, :cap]
    two[...] = got[:, cap:]


def interface_values(blocks, steps, counts, interface, us, after=()):
    rows = blocks[0].shape[0]
    total = sum(block.shape[1] for block in blocks)
    cap = interface.shape[1] // 2
    given, places = operands(blocks)
    return pl.pallas_call(
        functools.partial(interface_kernel, places, steps),
        in_specs=[smem] + [vmem] * (1 + len(given)) + [anywhere] * len(after),
        out_shape=[jax.ShapeDtypeStruct((rows, cap), f32)] * 2,
        scratch_shapes=[pltpu.VMEM((total, 2 * cap), bf16)],
        compiler_params=params(),
        cost_estimate=cost(us),
        name="interface_values",
    )(counts, interface, *given, *after)


def picked_kernel(places, hot, *refs):
    picked_values(views(places, refs), hot, *refs[-2:])


def picked(blocks, hot):
    rows = blocks[0].shape[0]
    given, places = operands(blocks)
    return pl.pallas_call(
        functools.partial(picked_kernel, places),
        in_specs=[vmem] * (1 + len(given)),
        out_shape=[jax.ShapeDtypeStruct((rows, hot.shape[1] // 2), f32)] * 2,
        compiler_params=params(),
        cost_estimate=cost(1),
        name="picked",
    )(hot, *given)


def tile_ids(conn, live, at, tile):
    ids = conn[:, at * tile : (at + 1) * tile]
    element = at * tile + lax.broadcasted_iota(jnp.int32, ids.shape, 1)
    return jnp.where(element < live[0], ids, -1)


def fill_gather(hot, conn, blocks, bases, tile):
    row = 0
    for at, block in enumerate(blocks):
        size = block.shape[1]
        iota = lax.broadcasted_iota(jnp.int32, (size, tile), 0)
        for corner in range(6):
            hot[row : row + size, corner * tile : (corner + 1) * tile] = one_hot(
                iota, conn[corner : corner + 1, :] - bases[at]
            )
        row += size


def fill_values(values, blocks):
    column = 0
    for block in blocks:
        size = block.shape[1]
        values[:, column : column + size] = split_rows(block[...])
        column += size


def magnetic_terms_kernel(places, mode_dev, live, conn, stiffness, mass_r, *refs):
    blocks = views(places, refs)
    out, done, values, hots, operator = refs[-5:]
    tile = operator.shape[2]
    done[...] = jnp.zeros_like(done)
    fill_values(values, blocks)
    bases = [0]
    for block in blocks[:-1]:
        bases.append(bases[-1] + block.shape[1])
    lane = lax.broadcasted_iota(jnp.int32, (8, tile), 0)
    squares = (own_member() * mode_dev + lax.rem(lane, mode_dev)).astype(f32) ** 2
    for step in range(out.shape[0]):
        hot = hots.at[step % 2]
        ids = by_partner(tile_ids(conn, live, step, tile), bases[1], blocks[1].shape[1])
        fill_gather(hot, ids, blocks, bases, tile)
        got = halves_sum(jnp.dot(values[...], hot[...], preferred_element_type=f32))
        at = slice(step * tile, (step + 1) * tile)
        for a in range(6):
            for b in range(6):
                operator[a * 6 + b] = diffusivity * (
                    stiffness[a, b : b + 1, at] + squares * mass_r[a, b : b + 1, at]
                )
        for low in range(0, out.shape[1], 8):
            for a in range(6):
                total = None
                for b in range(6):
                    term = operator[a * 6 + b] * got[low : low + 8, b * tile : (b + 1) * tile]
                    total = term if total is None else total + term
                out[step, low : low + 8, a * tile : (a + 1) * tile] = total


def magnetic_terms(blocks, mode_dev, live, conn, stiffness, mass_r, after):
    rows = blocks[0].shape[0]
    elems = conn.shape[1]
    tile = ELEM_TILE
    total = sum(block.shape[1] for block in blocks)
    given, places = operands(blocks)
    return pl.pallas_call(
        functools.partial(magnetic_terms_kernel, places, mode_dev),
        in_specs=[smem] + [vmem] * (3 + len(given)) + [anywhere] * len(after),
        out_shape=[
            jax.ShapeDtypeStruct((elems // tile, rows, 6 * tile), f32),
            jax.ShapeDtypeStruct((8, 128), f32),
        ],
        scratch_shapes=[
            pltpu.VMEM((2 * rows, total), bf16),
            pltpu.VMEM((2, total, 6 * tile), bf16),
            pltpu.VMEM((36, 8, tile), f32),
        ],
        compiler_params=params(28 << 20),
        cost_estimate=cost(30),
        name="magnetic_terms",
    )(live, conn, stiffness, mass_r, *given, *after)


def gather_kernel(places, steps, live, conn, *refs):
    blocks = views(places, refs)
    out, values, hots = refs[-3:]
    tile = out.shape[2] // 6
    fill_values(values, blocks)
    bases = [base_of(step, block.shape[1]) for step, block in zip(steps, blocks)]
    for step in range(out.shape[0]):
        hot = hots.at[step % 2]
        fill_gather(hot, tile_ids(conn, live, step, tile), blocks, bases, tile)
        out[step] = halves_sum(jnp.dot(values[...], hot[...], preferred_element_type=f32))


def gathered(blocks, steps, live, conn):
    rows = blocks[0].shape[0]
    elems = conn.shape[1]
    tile = ELEM_TILE
    total = sum(block.shape[1] for block in blocks)
    given, places = operands(blocks)
    return pl.pallas_call(
        functools.partial(gather_kernel, places, steps),
        in_specs=[smem] + [vmem] * (1 + len(given)),
        out_shape=jax.ShapeDtypeStruct((elems // tile, rows, 6 * tile), f32),
        scratch_shapes=[
            pltpu.VMEM((2 * rows, total), bf16),
            pltpu.VMEM((2, total, 6 * tile), bf16),
        ],
        compiler_params=params(28 << 20),
        cost_estimate=cost(5),
        name="gathered",
    )(live, conn, *given)


def fill_scatter(hot, conn_columns, first, tile):
    iota = lax.broadcasted_iota(jnp.int32, (tile, hot.shape[1]), 1)
    for corner in range(6):
        hot[corner * tile : (corner + 1) * tile, :] = one_hot(
            iota, conn_columns[:, corner : corner + 1] - first
        )


def ghost_terms_kernel(
    first, live, conn, coupling, magnetic_part, electric_part, left, right,
    terms, left_sums, right_sums, values, hots, hots_columns
):
    tile = terms.shape[2] // 6
    rows, cap = left.shape
    fill_values(values, (left, right))
    sums = None
    for step in range(terms.shape[0]):
        hot, hot_columns = hots.at[step % 2], hots_columns.at[step % 2]
        ids = by_partner(tile_ids(conn, live, step, tile), first, cap)
        fill_gather(hot, ids, (left, right), (first, first + cap), tile)
        fill_scatter(hot_columns, columns_of(ids), first, tile)
        got = electric_part[step] + halves_sum(
            jnp.dot(values[...], hot[...], preferred_element_type=f32)
        )
        across = slice(step * tile, (step + 1) * tile)
        for low in range(0, rows, 16):
            for a in range(6):
                at = slice(a * tile, (a + 1) * tile)
                total = -magnetic_part[step, low : low + 16, at]
                for b in range(6):
                    total = total + coupling[a, b : b + 1, across] * got[low : low + 16, b * tile : (b + 1) * tile]
                high = total.astype(bf16)
                terms[step, low : low + 16, at] = high
                terms[step, rows + low : rows + low + 16, at] = (total - high.astype(f32)).astype(bf16)
        part = halves_sum(jnp.dot(terms[step], hot_columns[...], preferred_element_type=f32))
        if step == 0:
            left_sums[...] = part[:, :cap]
            right_sums[...] = part[:, cap:]
        else:
            left_sums[...] += part[:, :cap]
            right_sums[...] += part[:, cap:]


def ghost_terms(first, live, conn, coupling, magnetic_part, electric_part, left, right):
    rows, cap = left.shape
    steps, _, wide = electric_part.shape
    return pl.pallas_call(
        functools.partial(ghost_terms_kernel, first),
        in_specs=[smem] + [vmem] * 6,
        out_shape=[
            jax.ShapeDtypeStruct((steps, 2 * rows, wide), bf16),
            jax.ShapeDtypeStruct((rows, cap), f32),
            jax.ShapeDtypeStruct((rows, cap), f32),
        ],
        scratch_shapes=[
            pltpu.VMEM((2 * rows, 2 * cap), bf16),
            pltpu.VMEM((2, 2 * cap, wide), bf16),
            pltpu.VMEM((2, wide, 2 * cap), bf16),
        ],
        compiler_params=params(),
        cost_estimate=cost(8),
        name="ghost_terms",
    )(live, conn, coupling, magnetic_part, electric_part, left, right)


def own_sums_kernel(live, conn, terms, out, hots):
    tile = terms.shape[2] // 6
    for step in range(terms.shape[0]):
        hot = hots.at[step % 2]
        fill_scatter(hot, columns_of(tile_ids(conn, live, step, tile)), 0, tile)
        part = halves_sum(jnp.dot(terms[step], hot[...], preferred_element_type=f32))
        if step == 0:
            out[...] = part
        else:
            out[...] += part


def own_sums(live, conn, terms, nodes):
    rows, wide = terms.shape[1] // 2, terms.shape[2]
    return pl.pallas_call(
        own_sums_kernel,
        in_specs=[smem, vmem, vmem],
        out_shape=jax.ShapeDtypeStruct((rows, nodes), f32),
        scratch_shapes=[pltpu.VMEM((2, wide, nodes), bf16)],
        compiler_params=params(),
        cost_estimate=cost(9),
        name="own_sums",
    )(live, conn, terms)


def interface_hot_kernel(steps, counts, interface, by_slot, by_node):
    ids = interface_ids(interface, counts)
    iota = lax.broadcasted_iota(jnp.int32, by_slot.shape, 1)
    by_slot[...] = one_hot(iota, columns_of(ids)[:, :1])
    member_hot(by_node, ids, steps, by_node.shape[0] // len(steps))


def interface_hot(counts, interface, nodes, steps):
    slots = interface.shape[1]
    return pl.pallas_call(
        functools.partial(interface_hot_kernel, steps),
        in_specs=[smem, vmem],
        out_shape=[
            jax.ShapeDtypeStruct((slots, nodes), bf16),
            jax.ShapeDtypeStruct((nodes, slots), bf16),
        ],
        compiler_params=params(),
        cost_estimate=cost(2),
        name="interface_hot",
    )(counts, interface)


def finish_kernel(hot, magnetic, sums, left, right, inv_mass, out, parts, sems):
    values = jnp.concatenate([split_rows(left[...]), split_rows(right[...])], 1)
    count, _, width = parts.shape
    copies = []
    for part in range(count):
        at = slice(part * width, (part + 1) * width)
        extra = halves_sum(jnp.dot(values, hot[:, at], preferred_element_type=f32))
        parts[part] = magnetic[:, at] + time_step * inv_mass[:, at] * (sums[:, at] + extra)
        copies.append(pltpu.make_async_copy(parts.at[part], out.at[:, at], sems.at[part]))
        copies[-1].start()
    for copy in copies:
        copy.wait()


def finish(hot, magnetic, sums, left, right, inv_mass):
    rows, nodes = magnetic.shape
    count = 4
    return pl.pallas_call(
        finish_kernel,
        in_specs=[vmem] * 6,
        out_specs=anywhere,
        out_shape=jax.ShapeDtypeStruct((rows, nodes), f32),
        scratch_shapes=[
            pltpu.VMEM((count, rows, nodes // count), f32),
            pltpu.SemaphoreType.DMA((count,)),
        ],
        compiler_params=params(),
        cost_estimate=cost(2),
        name="finish",
    )(hot, magnetic, sums, left, right, inv_mass)


def between_chips(blocks):
    members = lax.axis_size("mode")
    order = sorted(range(1, members // 2), key=lambda t: -t)
    got = {
        t: lax.ppermute(blocks[t], "mode", [(k, k ^ (2 * t)) for k in range(members)])
        for t in order
    }
    return [blocks[0]] + [got[t] for t in range(1, members // 2)]


def between_cores(blocks, after):
    members = lax.axis_size("mode")
    return lax.ppermute(lower_halves(blocks, after), "mode", [(k, k ^ 1) for k in range(members)])


def neighbours(one, two):
    count = lax.axis_size("mesh")
    got = []
    for values, start in ((one, 0), (two, 1)):
        lower = range(start, count - 1, 2)
        pairs = [(i, i + 1) for i in lower] + [(i + 1, i) for i in lower]
        got.append(lax.ppermute(values, "mesh", pairs))
    return got


def on_device(
    magnetic, velocity, stiffness, mass_r, coupling, inv_mass, connect, interface, counts, elem_live
):
    fields, vector_parts, mode_dev, node_dev = magnetic.shape
    rows = fields * vector_parts * mode_dev
    cap = interface.shape[1] // 2
    members = lax.axis_size("mode")
    slab = node_dev // members
    values = magnetic.reshape(rows, node_dev)

    far = pack(values, tuple(range(2, members // 2)), slab, ())
    near = pack(values, (0, 1), slab, (far[0],))
    packed = near + far
    kept = between_chips(packed)
    own = Block(values, rows)
    mag_left, mag_right = neighbours(
        *interface_values([own], (None,), counts, interface, 1, (packed[0],))
    )
    extended = [own, Block(mag_left, rows), Block(mag_right, rows)]
    steps = tuple(range(members))
    hot, node_hot = interface_hot(counts, interface, node_dev, steps)
    swapped = between_cores(kept, (mag_left, mag_right, hot))
    arrived = []
    for t, block in enumerate(kept):
        arrived += [Block(block, rows), Block(swapped, rows, t)]
    inverse, forward = transform_tables(mode_dev, members)
    sent = list(transform(arrived, velocity, inverse, forward, mode_dev, fields))
    sent[1] = relay(sent[1], (sent[2],))
    kept = between_chips(sent)
    magnetic_part, done = magnetic_terms(
        extended, mode_dev, elem_live, connect, stiffness, mass_r, (sent[1],)
    )
    electric = []
    swapped = between_cores(kept[:2], (done,))
    for t, block in enumerate(kept[:2]):
        electric += [Block(block, rows), Block(swapped, rows, t)]
    swapped = between_cores(kept[2:], ())
    for t, block in enumerate(kept[2:]):
        electric += [Block(block, rows), Block(swapped, rows, t)]
    ele_left, ele_right = neighbours(*picked(electric, node_hot))
    electric_part = gathered(electric, steps, elem_live, connect)
    terms, left_sums, right_sums = ghost_terms(
        node_dev, elem_live, connect, coupling, magnetic_part, electric_part, ele_left, ele_right
    )
    sum_left, sum_right = neighbours(left_sums, right_sums)
    sums = own_sums(elem_live, connect, terms, node_dev)
    out = finish(hot, values, sums, sum_left, sum_right, inv_mass[None, :])
    return out.reshape(magnetic.shape)


def solution(mesh):
    return jax.shard_map(
        on_device,
        mesh=mesh,
        in_specs=(
            P(None, None, "mode", "mesh"),
            P(None, None, ("mesh", "mode")),
            P(None, None, "mesh"),
            P(None, None, "mesh"),
            P(None, None, "mesh"),
            P("mesh"),
            P(None, "mesh"),
            P("mesh", None),
            P("mesh", None),
            P("mesh"),
        ),
        out_specs=P(None, None, "mode", "mesh"),
        check_vma=False,
    )
```

```python
import functools
import math

import jax
import jax.numpy as jnp
import numpy as np
from jax import lax
from jax.experimental import pallas as pl
from jax.experimental.pallas import tpu as pltpu
from jax.sharding import PartitionSpec as P

diffusivity = 1.0
time_step = 0.1
f32 = jnp.float32
bf16 = jnp.bfloat16
KERNEL_VMEM = 20 << 20
ELEM_TILE = 256


def whole_block(shape):
    return pl.BlockSpec(shape, lambda *ids: (0,) * len(shape))


class Block:
    def __init__(self, array, rows, at=0):
        self.array, self.rows, self.at = array, rows, at
        self.shape = (rows, array.shape[1])

    def spec(self):
        at = self.at
        return pl.BlockSpec(self.shape, lambda *ids: (at, 0))


def specs(blocks):
    return [block.spec() for block in blocks]


def arrays(blocks):
    return [block.array for block in blocks]


def operands(blocks):
    given, places = [], []
    for block in blocks:
        found = [array is block.array for array in given]
        if True not in found:
            found.append(True)
            given.append(block.array)
        places.append((found.index(True), block.at * block.rows, block.rows))
    return given, tuple(places)


def views(places, refs):
    return [refs[at].at[low : low + rows, :] for at, low, rows in places]


vmem = pl.BlockSpec(memory_space=pltpu.VMEM)
smem = pl.BlockSpec(memory_space=pltpu.SMEM)
anywhere = pl.BlockSpec(memory_space=pl.ANY)


def params(vmem=KERNEL_VMEM):
    return pltpu.CompilerParams(vmem_limit_bytes=vmem)


def cost(us):
    return pl.CostEstimate(flops=0, bytes_accessed=int(us * 3.0e6), transcendentals=0)


def split_rows(value):
    high = value.astype(bf16)
    low = (value - high.astype(f32)).astype(bf16)
    return jnp.concatenate([high, low], 0)


def halves_sum(value):
    rows = value.shape[0] // 2
    return value[:rows] + value[rows:]


def own_member():
    return lax.axis_index("mode")


def base_of(step, slab):
    return (own_member() ^ step) * slab


def columns_of(ids):
    rows = ids.shape[0]
    filled = jnp.concatenate([ids, jnp.broadcast_to(ids[:1], (8 - rows, ids.shape[1]))], 0)
    return filled.T


def one_hot(iota, ids):
    return jnp.where(iota == ids, 1.0, 0.0).astype(bf16)


def transform_tables(mode_dev, members):
    spectral_modes = mode_dev * members
    samples = 2 * spectral_modes
    row = np.arange(samples)
    parity = (row // mode_dev) % 2
    mode = row // (2 * mode_dev) * mode_dev + row % mode_dev
    phases = 2.0 * np.pi / samples * (np.arange(samples)[None, :] * mode[:, None] % samples)
    inverse = np.where(parity[:, None] == 0, np.cos(phases), np.sin(phases))
    weights = np.where((mode == 0) & (parity == 0), 1.0, 2.0) / samples
    return jnp.asarray(inverse, f32), jnp.asarray(inverse * weights[:, None], f32)


def spread_table(table):
    high = table.astype(bf16)
    low = (table - high.astype(f32)).astype(bf16)
    return jnp.concatenate([high, high, low], 1)


def spread_value(value):
    high = value.astype(bf16)
    low = (value - high.astype(f32)).astype(bf16)
    return jnp.concatenate([high, low, high], 0)


def transform_kernel(places, mode_dev, fields, *refs):
    inverse, forward, velocity = refs[:3]
    blocks = views(places, refs[3:])
    members = len(blocks)
    outs = refs[-(members // 2) :]
    pair = 2 * mode_dev
    rows = blocks[0].shape[0]
    ordered = []
    for table in (inverse, forward):
        starts = [pl.multiple_of(base_of(step, pair), 8) for step in range(members)]
        ordered.append(jnp.concatenate([table[pl.ds(start, pair), :] for start in starts], 0))
    to_points, to_modes = spread_table(ordered[0].T), spread_table(ordered[1])
    for field in range(fields):
        points = []
        for part in range(3):
            low = (field * 3 + part) * pair
            stacked = jnp.concatenate([block[low : low + pair, :] for block in blocks], 0)
            points.append(
                jnp.dot(to_points, spread_value(stacked), preferred_element_type=f32)
            )
        for part in range(3):
            after, last = (part + 1) % 3, (part + 2) % 3
            cross = velocity[after] * points[last] - velocity[last] * points[after]
            back = jnp.dot(to_modes, spread_value(cross), preferred_element_type=f32)
            low = (field * 3 + part) * pair
            for step in range(members):
                at = (step % 2) * rows + low
                outs[step // 2][at : at + pair, :] = back[step * pair : (step + 1) * pair]


def transform(blocks, velocity, inverse, forward, mode_dev, fields):
    members = len(blocks)
    rows, slab = blocks[0].shape
    given, places = operands(blocks)
    return pl.pallas_call(
        functools.partial(transform_kernel, places, mode_dev, fields),
        in_specs=[vmem] * (3 + len(given)),
        out_shape=[jax.ShapeDtypeStruct((2 * rows, slab), f32)] * (members // 2),
        compiler_params=params(),
        cost_estimate=cost(1),
        name="transform",
    )(inverse, forward, velocity, *given)


def pack_kernel(chips, rows, slab, values, *refs):
    outs, sems = refs[-1 - len(chips) : -1], refs[-1]
    copies = []
    for at in range(2 * len(chips)):
        start = pl.multiple_of(base_of(2 * chips[at // 2] + at % 2, slab), 128)
        half = at % 2
        copies.append(
            pltpu.make_async_copy(
                values.at[:, pl.ds(start, slab)],
                outs[at // 2].at[half * rows : (half + 1) * rows, :],
                sems.at[at],
            )
        )
    for copy in copies:
        copy.start()
    for copy in copies:
        copy.wait()


def pack(values, chips, slab, after):
    rows = values.shape[0]
    anywhere = pl.BlockSpec(memory_space=pl.ANY)
    return pl.pallas_call(
        functools.partial(pack_kernel, chips, rows, slab),
        in_specs=[pl.BlockSpec(memory_space=pltpu.HBM)] + [anywhere] * len(after),
        out_specs=[anywhere] * len(chips),
        out_shape=[jax.ShapeDtypeStruct((2 * rows, slab), f32)] * len(chips),
        scratch_shapes=[pltpu.SemaphoreType.DMA((2 * len(chips),))],
        compiler_params=params(),
        cost_estimate=cost(0.5),
        name="pack",
    )(values, *after)


def relay_kernel(source, *refs):
    copy = pltpu.make_async_copy(source, refs[-2], refs[-1])
    copy.start()
    copy.wait()


def relay(source, after):
    anywhere = pl.BlockSpec(memory_space=pl.ANY)
    return pl.pallas_call(
        relay_kernel,
        in_specs=[anywhere] * (1 + len(after)),
        out_specs=anywhere,
        out_shape=jax.ShapeDtypeStruct(source.shape, f32),
        scratch_shapes=[pltpu.SemaphoreType.DMA],
        compiler_params=params(),
        cost_estimate=cost(0.5),
        name="relay",
    )(source, *after)


def lower_halves_kernel(count, *refs):
    blocks, out, sems = refs[:count], refs[-2], refs[-1]
    rows = blocks[0].shape[0] // 2
    copies = [
        pltpu.make_async_copy(
            block.at[rows:, :], out.at[at * rows : (at + 1) * rows, :], sems.at[at]
        )
        for at, block in enumerate(blocks)
    ]
    for copy in copies:
        copy.start()
    for copy in copies:
        copy.wait()


def lower_halves(blocks, after):
    rows, width = blocks[0].shape[0] // 2, blocks[0].shape[1]
    anywhere = pl.BlockSpec(memory_space=pl.ANY)
    return pl.pallas_call(
        functools.partial(lower_halves_kernel, len(blocks)),
        in_specs=[anywhere] * (len(blocks) + len(after)),
        out_specs=anywhere,
        out_shape=jax.ShapeDtypeStruct((len(blocks) * rows, width), f32),
        scratch_shapes=[pltpu.SemaphoreType.DMA((len(blocks),))],
        compiler_params=params(),
        cost_estimate=cost(0.01),
        name="lower_halves",
    )(*blocks, *after)


def even_partition():
    return lax.rem(lax.axis_index("mesh"), 2) == 0


def interface_ids(interface, counts):
    width = interface.shape[1]
    cap = width // 2
    lists = jnp.broadcast_to(interface[...], (8, width))
    shifted = pltpu.roll(lists, lax.rem(width - counts[0, 0], width), 1)
    left, right = lists[:1, :cap], shifted[:1, :cap]
    even = even_partition()
    return jnp.concatenate([jnp.where(even, right, left), jnp.where(even, left, right)], 1)


def by_partner(ids, first, cap):
    swapped = jnp.where(ids < first + cap, ids + cap, ids - cap)
    return jnp.where((ids >= first) & even_partition(), swapped, ids)


def member_hot(out, ids, steps, slab):
    for at, step in enumerate(steps):
        iota = lax.broadcasted_iota(jnp.int32, (slab, ids.shape[1]), 0)
        base = 0 if step is None else base_of(step, slab)
        out[at * slab : (at + 1) * slab, :] = one_hot(iota, ids - base)


def interface_kernel(places, steps, counts, interface, *refs):
    one, two, hot = refs[-3:]
    blocks = views(places, refs)
    member_hot(hot, interface_ids(interface, counts), steps, blocks[0].shape[1])
    picked_values(blocks, hot, one, two)


def picked_values(blocks, hot, one, two):
    cap = one.shape[1]
    values = jnp.concatenate([split_rows(block[...]) for block in blocks], 1)
    got = halves_sum(jnp.dot(values, hot[...], preferred_element_type=f32))
    one[...] = got[:, :cap]
    two[...] = got[:, cap:]


def interface_values(blocks, steps, counts, interface, us, after=()):
    rows = blocks[0].shape[0]
    total = sum(block.shape[1] for block in blocks)
    cap = interface.shape[1] // 2
    given, places = operands(blocks)
    return pl.pallas_call(
        functools.partial(interface_kernel, places, steps),
        in_specs=[smem] + [vmem] * (1 + len(given)) + [anywhere] * len(after),
        out_shape=[jax.ShapeDtypeStruct((rows, cap), f32)] * 2,
        scratch_shapes=[pltpu.VMEM((total, 2 * cap), bf16)],
        compiler_params=params(),
        cost_estimate=cost(us),
        name="interface_values",
    )(counts, interface, *given, *after)


def picked_kernel(places, hot, *refs):
    picked_values(views(places, refs), hot, *refs[-2:])


def picked(blocks, hot):
    rows = blocks[0].shape[0]
    given, places = operands(blocks)
    return pl.pallas_call(
        functools.partial(picked_kernel, places),
        in_specs=[vmem] * (1 + len(given)),
        out_shape=[jax.ShapeDtypeStruct((rows, hot.shape[1] // 2), f32)] * 2,
        compiler_params=params(),
        cost_estimate=cost(1),
        name="picked",
    )(hot, *given)


def tile_ids(conn, live, at, tile):
    ids = conn[:, at * tile : (at + 1) * tile]
    element = at * tile + lax.broadcasted_iota(jnp.int32, ids.shape, 1)
    return jnp.where(element < live[0], ids, -1)


def fill_gather(hot, conn, blocks, bases, tile):
    row = 0
    for at, block in enumerate(blocks):
        size = block.shape[1]
        iota = lax.broadcasted_iota(jnp.int32, (size, tile), 0)
        for corner in range(6):
            hot[row : row + size, corner * tile : (corner + 1) * tile] = one_hot(
                iota, conn[corner : corner + 1, :] - bases[at]
            )
        row += size


def fill_values(values, blocks):
    column = 0
    for block in blocks:
        size = block.shape[1]
        values[:, column : column + size] = split_rows(block[...])
        column += size


def magnetic_terms_kernel(places, mode_dev, live, conn, stiffness, mass_r, *refs):
    blocks = views(places, refs)
    out, done, values, hots, operator = refs[-5:]
    tile = operator.shape[2]
    done[...] = jnp.zeros_like(done)
    fill_values(values, blocks)
    bases = [0]
    for block in blocks[:-1]:
        bases.append(bases[-1] + block.shape[1])
    lane = lax.broadcasted_iota(jnp.int32, (8, tile), 0)
    squares = (own_member() * mode_dev + lax.rem(lane, mode_dev)).astype(f32) ** 2
    for step in range(out.shape[0]):
        hot = hots.at[step % 2]
        ids = by_partner(tile_ids(conn, live, step, tile), bases[1], blocks[1].shape[1])
        fill_gather(hot, ids, blocks, bases, tile)
        got = halves_sum(jnp.dot(values[...], hot[...], preferred_element_type=f32))
        at = slice(step * tile, (step + 1) * tile)
        for a in range(6):
            for b in range(6):
                operator[a * 6 + b] = diffusivity * (
                    stiffness[a, b : b + 1, at] + squares * mass_r[a, b : b + 1, at]
                )
        for low in range(0, out.shape[1], 8):
            for a in range(6):
                total = None
                for b in range(6):
                    term = operator[a * 6 + b] * got[low : low + 8, b * tile : (b + 1) * tile]
                    total = term if total is None else total + term
                out[step, low : low + 8, a * tile : (a + 1) * tile] = total


def magnetic_terms(blocks, mode_dev, live, conn, stiffness, mass_r, after):
    rows = blocks[0].shape[0]
    elems = conn.shape[1]
    tile = ELEM_TILE
    total = sum(block.shape[1] for block in blocks)
    given, places = operands(blocks)
    return pl.pallas_call(
        functools.partial(magnetic_terms_kernel, places, mode_dev),
        in_specs=[smem] + [vmem] * (3 + len(given)) + [anywhere] * len(after),
        out_shape=[
            jax.ShapeDtypeStruct((elems // tile, rows, 6 * tile), f32),
            jax.ShapeDtypeStruct((8, 128), f32),
        ],
        scratch_shapes=[
            pltpu.VMEM((2 * rows, total), bf16),
            pltpu.VMEM((2, total, 6 * tile), bf16),
            pltpu.VMEM((36, 8, tile), f32),
        ],
        compiler_params=params(28 << 20),
        cost_estimate=cost(30),
        name="magnetic_terms",
    )(live, conn, stiffness, mass_r, *given, *after)


def gather_kernel(places, steps, live, conn, *refs):
    blocks = views(places, refs)
    out, values, hots = refs[-3:]
    tile = out.shape[2] // 6
    fill_values(values, blocks)
    bases = [base_of(step, block.shape[1]) for step, block in zip(steps, blocks)]
    for step in range(out.shape[0]):
        hot = hots.at[step % 2]
        fill_gather(hot, tile_ids(conn, live, step, tile), blocks, bases, tile)
        out[step] = halves_sum(jnp.dot(values[...], hot[...], preferred_element_type=f32))


def gathered(blocks, steps, live, conn):
    rows = blocks[0].shape[0]
    elems = conn.shape[1]
    tile = ELEM_TILE
    total = sum(block.shape[1] for block in blocks)
    given, places = operands(blocks)
    return pl.pallas_call(
        functools.partial(gather_kernel, places, steps),
        in_specs=[smem] + [vmem] * (1 + len(given)),
        out_shape=jax.ShapeDtypeStruct((elems // tile, rows, 6 * tile), f32),
        scratch_shapes=[
            pltpu.VMEM((2 * rows, total), bf16),
            pltpu.VMEM((2, total, 6 * tile), bf16),
        ],
        compiler_params=params(28 << 20),
        cost_estimate=cost(5),
        name="gathered",
    )(live, conn, *given)


def fill_scatter(hot, conn_columns, first, tile):
    iota = lax.broadcasted_iota(jnp.int32, (tile, hot.shape[1]), 1)
    for corner in range(6):
        hot[corner * tile : (corner + 1) * tile, :] = one_hot(
            iota, conn_columns[:, corner : corner + 1] - first
        )


def ghost_hot_kernel(first, live, conn, by_slot, by_corner):
    slots, tile = by_slot.shape[1], by_slot.shape[2] // 6
    for step in range(by_slot.shape[0]):
        ids = by_partner(tile_ids(conn, live, step, tile), first, slots // 2)
        iota = lax.broadcasted_iota(jnp.int32, (slots, tile), 0)
        for corner in range(6):
            by_slot[step, :, corner * tile : (corner + 1) * tile] = one_hot(
                iota, ids[corner : corner + 1, :] - first
            )
        fill_scatter(by_corner.at[step], columns_of(ids), first, tile)


def ghost_hot(first, slots, live, conn):
    wide = 6 * ELEM_TILE
    steps = conn.shape[1] // ELEM_TILE
    return pl.pallas_call(
        functools.partial(ghost_hot_kernel, first),
        in_specs=[smem, vmem],
        out_shape=[
            jax.ShapeDtypeStruct((steps, slots, wide), bf16),
            jax.ShapeDtypeStruct((steps, wide, slots), bf16),
        ],
        compiler_params=params(),
        cost_estimate=cost(3),
        name="ghost_hot",
    )(live, conn)


def ghost_terms_kernel(
    hots, hots_columns, coupling, magnetic_part, electric_part, left, right,
    terms, left_sums, right_sums, values
):
    tile = terms.shape[2] // 6
    rows, cap = left.shape
    fill_values(values, (left, right))
    sums = None
    for step in range(terms.shape[0]):
        got = electric_part[step] + halves_sum(
            jnp.dot(values[...], hots[step], preferred_element_type=f32)
        )
        across = slice(step * tile, (step + 1) * tile)
        for low in range(0, rows, 16):
            for a in range(6):
                at = slice(a * tile, (a + 1) * tile)
                total = -magnetic_part[step, low : low + 16, at]
                for b in range(6):
                    total = total + coupling[a, b : b + 1, across] * got[low : low + 16, b * tile : (b + 1) * tile]
                high = total.astype(bf16)
                terms[step, low : low + 16, at] = high
                terms[step, rows + low : rows + low + 16, at] = (total - high.astype(f32)).astype(bf16)
        part = halves_sum(jnp.dot(terms[step], hots_columns[step], preferred_element_type=f32))
        if step == 0:
            left_sums[...] = part[:, :cap]
            right_sums[...] = part[:, cap:]
        else:
            left_sums[...] += part[:, :cap]
            right_sums[...] += part[:, cap:]


def ghost_terms(hots, coupling, magnetic_part, electric_part, left, right):
    rows, cap = left.shape
    steps, _, wide = electric_part.shape
    return pl.pallas_call(
        ghost_terms_kernel,
        in_specs=[vmem] * 7,
        out_shape=[
            jax.ShapeDtypeStruct((steps, 2 * rows, wide), bf16),
            jax.ShapeDtypeStruct((rows, cap), f32),
            jax.ShapeDtypeStruct((rows, cap), f32),
        ],
        scratch_shapes=[pltpu.VMEM((2 * rows, 2 * cap), bf16)],
        compiler_params=params(),
        cost_estimate=cost(8),
        name="ghost_terms",
    )(*hots, coupling, magnetic_part, electric_part, left, right)


def own_sums_kernel(live, conn, terms, out, hots):
    tile = terms.shape[2] // 6
    for step in range(terms.shape[0]):
        hot = hots.at[step % 2]
        fill_scatter(hot, columns_of(tile_ids(conn, live, step, tile)), 0, tile)
        part = halves_sum(jnp.dot(terms[step], hot[...], preferred_element_type=f32))
        if step == 0:
            out[...] = part
        else:
            out[...] += part


def own_sums(live, conn, terms, nodes):
    rows, wide = terms.shape[1] // 2, terms.shape[2]
    return pl.pallas_call(
        own_sums_kernel,
        in_specs=[smem, vmem, vmem],
        out_shape=jax.ShapeDtypeStruct((rows, nodes), f32),
        scratch_shapes=[pltpu.VMEM((2, wide, nodes), bf16)],
        compiler_params=params(),
        cost_estimate=cost(9),
        name="own_sums",
    )(live, conn, terms)


def interface_hot_kernel(steps, counts, interface, by_slot, by_node):
    ids = interface_ids(interface, counts)
    iota = lax.broadcasted_iota(jnp.int32, by_slot.shape, 1)
    by_slot[...] = one_hot(iota, columns_of(ids)[:, :1])
    member_hot(by_node, ids, steps, by_node.shape[0] // len(steps))


def interface_hot(counts, interface, nodes, steps):
    slots = interface.shape[1]
    return pl.pallas_call(
        functools.partial(interface_hot_kernel, steps),
        in_specs=[smem, vmem],
        out_shape=[
            jax.ShapeDtypeStruct((slots, nodes), bf16),
            jax.ShapeDtypeStruct((nodes, slots), bf16),
        ],
        compiler_params=params(),
        cost_estimate=cost(2),
        name="interface_hot",
    )(counts, interface)


def finish_kernel(hot, magnetic, sums, left, right, inv_mass, out, parts, sems):
    values = jnp.concatenate([split_rows(left[...]), split_rows(right[...])], 1)
    count, _, width = parts.shape
    copies = []
    for part in range(count):
        at = slice(part * width, (part + 1) * width)
        extra = halves_sum(jnp.dot(values, hot[:, at], preferred_element_type=f32))
        parts[part] = magnetic[:, at] + time_step * inv_mass[:, at] * (sums[:, at] + extra)
        copies.append(pltpu.make_async_copy(parts.at[part], out.at[:, at], sems.at[part]))
        copies[-1].start()
    for copy in copies:
        copy.wait()


def finish(hot, magnetic, sums, left, right, inv_mass):
    rows, nodes = magnetic.shape
    count = 4
    return pl.pallas_call(
        finish_kernel,
        in_specs=[vmem] * 6,
        out_specs=anywhere,
        out_shape=jax.ShapeDtypeStruct((rows, nodes), f32),
        scratch_shapes=[
            pltpu.VMEM((count, rows, nodes // count), f32),
            pltpu.SemaphoreType.DMA((count,)),
        ],
        compiler_params=params(),
        cost_estimate=cost(2),
        name="finish",
    )(hot, magnetic, sums, left, right, inv_mass)


def between_chips(blocks):
    members = lax.axis_size("mode")
    order = sorted(range(1, members // 2), key=lambda t: -t)
    got = {
        t: lax.ppermute(blocks[t], "mode", [(k, k ^ (2 * t)) for k in range(members)])
        for t in order
    }
    return [blocks[0]] + [got[t] for t in range(1, members // 2)]


def between_cores(blocks, after):
    members = lax.axis_size("mode")
    return lax.ppermute(lower_halves(blocks, after), "mode", [(k, k ^ 1) for k in range(members)])


def neighbours(one, two):
    count = lax.axis_size("mesh")
    got = []
    for values, start in ((one, 0), (two, 1)):
        lower = range(start, count - 1, 2)
        pairs = [(i, i + 1) for i in lower] + [(i + 1, i) for i in lower]
        got.append(lax.ppermute(values, "mesh", pairs))
    return got


def on_device(
    magnetic, velocity, stiffness, mass_r, coupling, inv_mass, connect, interface, counts, elem_live
):
    fields, vector_parts, mode_dev, node_dev = magnetic.shape
    rows = fields * vector_parts * mode_dev
    cap = interface.shape[1] // 2
    members = lax.axis_size("mode")
    slab = node_dev // members
    values = magnetic.reshape(rows, node_dev)

    far = pack(values, tuple(range(2, members // 2)), slab, ())
    near = pack(values, (0, 1), slab, (far[0],))
    packed = near + far
    kept = between_chips(packed)
    own = Block(values, rows)
    mag_left, mag_right = neighbours(
        *interface_values([own], (None,), counts, interface, 1, (packed[0],))
    )
    extended = [own, Block(mag_left, rows), Block(mag_right, rows)]
    steps = tuple(range(members))
    hot, node_hot = interface_hot(counts, interface, node_dev, steps)
    ghost_hots = ghost_hot(node_dev, 2 * cap, elem_live, connect)
    swapped = between_cores(kept, (mag_left, mag_right, hot, ghost_hots[0]))
    arrived = []
    for t, block in enumerate(kept):
        arrived += [Block(block, rows), Block(swapped, rows, t)]
    inverse, forward = transform_tables(mode_dev, members)
    sent = list(transform(arrived, velocity, inverse, forward, mode_dev, fields))
    sent[1] = relay(sent[1], (sent[2],))
    kept = between_chips(sent)
    magnetic_part, done = magnetic_terms(
        extended, mode_dev, elem_live, connect, stiffness, mass_r, (sent[1],)
    )
    electric = []
    swapped = between_cores(kept[:2], (done,))
    for t, block in enumerate(kept[:2]):
        electric += [Block(block, rows), Block(swapped, rows, t)]
    swapped = between_cores(kept[2:], ())
    for t, block in enumerate(kept[2:]):
        electric += [Block(block, rows), Block(swapped, rows, t)]
    ele_left, ele_right = neighbours(*picked(electric, node_hot))
    electric_part = gathered(electric, steps, elem_live, connect)
    terms, left_sums, right_sums = ghost_terms(
        ghost_hots, coupling, magnetic_part, electric_part, ele_left, ele_right
    )
    sum_left, sum_right = neighbours(left_sums, right_sums)
    sums = own_sums(elem_live, connect, terms, node_dev)
    out = finish(hot, values, sums, sum_left, sum_right, inv_mass[None, :])
    return out.reshape(magnetic.shape)


def solution(mesh):
    return jax.shard_map(
        on_device,
        mesh=mesh,
        in_specs=(
            P(None, None, "mode", "mesh"),
            P(None, None, ("mesh", "mode")),
            P(None, None, "mesh"),
            P(None, None, "mesh"),
            P(None, None, "mesh"),
            P("mesh"),
            P(None, "mesh"),
            P("mesh", None),
            P("mesh", None),
            P("mesh"),
        ),
        out_specs=P(None, None, "mode", "mesh"),
        check_vma=False,
    )
```

```python
import functools
import math

import jax
import jax.numpy as jnp
import numpy as np
from jax import lax
from jax.experimental import pallas as pl
from jax.experimental.pallas import tpu as pltpu
from jax.sharding import PartitionSpec as P

diffusivity = 1.0
time_step = 0.1
f32 = jnp.float32
bf16 = jnp.bfloat16
KERNEL_VMEM = 20 << 20
ELEM_TILE = 256


def whole_block(shape):
    return pl.BlockSpec(shape, lambda *ids: (0,) * len(shape))


class Block:
    def __init__(self, array, rows, at=0):
        self.array, self.rows, self.at = array, rows, at
        self.shape = (rows, array.shape[1])

    def spec(self):
        at = self.at
        return pl.BlockSpec(self.shape, lambda *ids: (at, 0))


def specs(blocks):
    return [block.spec() for block in blocks]


def arrays(blocks):
    return [block.array for block in blocks]


def operands(blocks):
    given, places = [], []
    for block in blocks:
        found = [array is block.array for array in given]
        if True not in found:
            found.append(True)
            given.append(block.array)
        places.append((found.index(True), block.at * block.rows, block.rows))
    return given, tuple(places)


def views(places, refs):
    return [refs[at].at[low : low + rows, :] for at, low, rows in places]


vmem = pl.BlockSpec(memory_space=pltpu.VMEM)
smem = pl.BlockSpec(memory_space=pltpu.SMEM)
anywhere = pl.BlockSpec(memory_space=pl.ANY)


def params(vmem=KERNEL_VMEM):
    return pltpu.CompilerParams(vmem_limit_bytes=vmem)


def cost(us):
    return pl.CostEstimate(flops=0, bytes_accessed=int(us * 3.0e6), transcendentals=0)


def split_rows(value):
    high = value.astype(bf16)
    low = (value - high.astype(f32)).astype(bf16)
    return jnp.concatenate([high, low], 0)


def halves_sum(value):
    rows = value.shape[0] // 2
    return value[:rows] + value[rows:]


def own_member():
    return lax.axis_index("mode")


def base_of(step, slab):
    return (own_member() ^ step) * slab


def columns_of(ids):
    rows = ids.shape[0]
    filled = jnp.concatenate([ids, jnp.broadcast_to(ids[:1], (8 - rows, ids.shape[1]))], 0)
    return filled.T


def one_hot(iota, ids):
    return jnp.where(iota == ids, 1.0, 0.0).astype(bf16)


def transform_tables(mode_dev, members):
    spectral_modes = mode_dev * members
    samples = 2 * spectral_modes
    row = np.arange(samples)
    parity = (row // mode_dev) % 2
    mode = row // (2 * mode_dev) * mode_dev + row % mode_dev
    phases = 2.0 * np.pi / samples * (np.arange(samples)[None, :] * mode[:, None] % samples)
    inverse = np.where(parity[:, None] == 0, np.cos(phases), np.sin(phases))
    weights = np.where((mode == 0) & (parity == 0), 1.0, 2.0) / samples
    return jnp.asarray(inverse, f32), jnp.asarray(inverse * weights[:, None], f32)


def spread_table(table):
    high = table.astype(bf16)
    low = (table - high.astype(f32)).astype(bf16)
    return jnp.concatenate([high, high, low], 1)


def spread_value(value):
    high = value.astype(bf16)
    low = (value - high.astype(f32)).astype(bf16)
    return jnp.concatenate([high, low, high], 0)


def transform_kernel(places, mode_dev, fields, *refs):
    inverse, forward, velocity = refs[:3]
    blocks = views(places, refs[3:])
    members = len(blocks)
    outs = refs[-(members // 2) :]
    pair = 2 * mode_dev
    rows = blocks[0].shape[0]
    ordered = []
    for table in (inverse, forward):
        starts = [pl.multiple_of(base_of(step, pair), 8) for step in range(members)]
        ordered.append(jnp.concatenate([table[pl.ds(start, pair), :] for start in starts], 0))
    to_points, to_modes = spread_table(ordered[0].T), spread_table(ordered[1])
    for field in range(fields):
        points = []
        for part in range(3):
            low = (field * 3 + part) * pair
            stacked = jnp.concatenate([block[low : low + pair, :] for block in blocks], 0)
            points.append(
                jnp.dot(to_points, spread_value(stacked), preferred_element_type=f32)
            )
        for part in range(3):
            after, last = (part + 1) % 3, (part + 2) % 3
            cross = velocity[after] * points[last] - velocity[last] * points[after]
            back = jnp.dot(to_modes, spread_value(cross), preferred_element_type=f32)
            low = (field * 3 + part) * pair
            for step in range(members):
                at = (step % 2) * rows + low
                outs[step // 2][at : at + pair, :] = back[step * pair : (step + 1) * pair]


def transform(blocks, velocity, inverse, forward, mode_dev, fields):
    members = len(blocks)
    rows, slab = blocks[0].shape
    given, places = operands(blocks)
    return pl.pallas_call(
        functools.partial(transform_kernel, places, mode_dev, fields),
        in_specs=[vmem] * (3 + len(given)),
        out_shape=[jax.ShapeDtypeStruct((2 * rows, slab), f32)] * (members // 2),
        compiler_params=params(),
        cost_estimate=cost(1),
        name="transform",
    )(inverse, forward, velocity, *given)


def pack_kernel(chips, rows, slab, values, *refs):
    outs, sems = refs[-1 - len(chips) : -1], refs[-1]
    copies = []
    for at in range(2 * len(chips)):
        start = pl.multiple_of(base_of(2 * chips[at // 2] + at % 2, slab), 128)
        half = at % 2
        copies.append(
            pltpu.make_async_copy(
                values.at[:, pl.ds(start, slab)],
                outs[at // 2].at[half * rows : (half + 1) * rows, :],
                sems.at[at],
            )
        )
    for copy in copies:
        copy.start()
    for copy in copies:
        copy.wait()


def pack(values, chips, slab, after):
    rows = values.shape[0]
    anywhere = pl.BlockSpec(memory_space=pl.ANY)
    return pl.pallas_call(
        functools.partial(pack_kernel, chips, rows, slab),
        in_specs=[pl.BlockSpec(memory_space=pltpu.HBM)] + [anywhere] * len(after),
        out_specs=[anywhere] * len(chips),
        out_shape=[jax.ShapeDtypeStruct((2 * rows, slab), f32)] * len(chips),
        scratch_shapes=[pltpu.SemaphoreType.DMA((2 * len(chips),))],
        compiler_params=params(),
        cost_estimate=cost(0.5),
        name="pack",
    )(values, *after)


def relay_kernel(source, *refs):
    copy = pltpu.make_async_copy(source, refs[-2], refs[-1])
    copy.start()
    copy.wait()


def relay(source, after):
    anywhere = pl.BlockSpec(memory_space=pl.ANY)
    return pl.pallas_call(
        relay_kernel,
        in_specs=[anywhere] * (1 + len(after)),
        out_specs=anywhere,
        out_shape=jax.ShapeDtypeStruct(source.shape, f32),
        scratch_shapes=[pltpu.SemaphoreType.DMA],
        compiler_params=params(),
        cost_estimate=cost(0.5),
        name="relay",
    )(source, *after)


def lower_halves_kernel(count, *refs):
    blocks, out, sems = refs[:count], refs[-2], refs[-1]
    rows = blocks[0].shape[0] // 2
    copies = [
        pltpu.make_async_copy(
            block.at[rows:, :], out.at[at * rows : (at + 1) * rows, :], sems.at[at]
        )
        for at, block in enumerate(blocks)
    ]
    for copy in copies:
        copy.start()
    for copy in copies:
        copy.wait()


def lower_halves(blocks, after):
    rows, width = blocks[0].shape[0] // 2, blocks[0].shape[1]
    anywhere = pl.BlockSpec(memory_space=pl.ANY)
    return pl.pallas_call(
        functools.partial(lower_halves_kernel, len(blocks)),
        in_specs=[anywhere] * (len(blocks) + len(after)),
        out_specs=anywhere,
        out_shape=jax.ShapeDtypeStruct((len(blocks) * rows, width), f32),
        scratch_shapes=[pltpu.SemaphoreType.DMA((len(blocks),))],
        compiler_params=params(),
        cost_estimate=cost(0.01),
        name="lower_halves",
    )(*blocks, *after)


def even_partition():
    return lax.rem(lax.axis_index("mesh"), 2) == 0


def interface_ids(interface, counts):
    width = interface.shape[1]
    cap = width // 2
    lists = jnp.broadcast_to(interface[...], (8, width))
    shifted = pltpu.roll(lists, lax.rem(width - counts[0, 0], width), 1)
    left, right = lists[:1, :cap], shifted[:1, :cap]
    even = even_partition()
    return jnp.concatenate([jnp.where(even, right, left), jnp.where(even, left, right)], 1)


def by_partner(ids, first, cap):
    swapped = jnp.where(ids < first + cap, ids + cap, ids - cap)
    return jnp.where((ids >= first) & even_partition(), swapped, ids)


def member_hot(out, ids, steps, slab):
    for at, step in enumerate(steps):
        iota = lax.broadcasted_iota(jnp.int32, (slab, ids.shape[1]), 0)
        base = 0 if step is None else base_of(step, slab)
        out[at * slab : (at + 1) * slab, :] = one_hot(iota, ids - base)


def interface_kernel(places, steps, counts, interface, *refs):
    one, two, hot = refs[-3:]
    blocks = views(places, refs)
    member_hot(hot, interface_ids(interface, counts), steps, blocks[0].shape[1])
    picked_values(blocks, hot, one, two)


def picked_values(blocks, hot, one, two):
    cap = one.shape[1]
    values = jnp.concatenate([split_rows(block[...]) for block in blocks], 1)
    got = halves_sum(jnp.dot(values, hot[...], preferred_element_type=f32))
    one[...] = got[:, :cap]
    two[...] = got[:, cap:]


def interface_values(blocks, steps, counts, interface, us, after=()):
    rows = blocks[0].shape[0]
    total = sum(block.shape[1] for block in blocks)
    cap = interface.shape[1] // 2
    given, places = operands(blocks)
    return pl.pallas_call(
        functools.partial(interface_kernel, places, steps),
        in_specs=[smem] + [vmem] * (1 + len(given)) + [anywhere] * len(after),
        out_shape=[jax.ShapeDtypeStruct((rows, cap), f32)] * 2,
        scratch_shapes=[pltpu.VMEM((total, 2 * cap), bf16)],
        compiler_params=params(),
        cost_estimate=cost(us),
        name="interface_values",
    )(counts, interface, *given, *after)


def picked_kernel(places, hot, *refs):
    picked_values(views(places, refs), hot, *refs[-2:])


def picked(blocks, hot):
    rows = blocks[0].shape[0]
    given, places = operands(blocks)
    return pl.pallas_call(
        functools.partial(picked_kernel, places),
        in_specs=[vmem] * (1 + len(given)),
        out_shape=[jax.ShapeDtypeStruct((rows, hot.shape[1] // 2), f32)] * 2,
        compiler_params=params(),
        cost_estimate=cost(1),
        name="picked",
    )(hot, *given)


def tile_ids(conn, live, at, tile):
    ids = conn[:, at * tile : (at + 1) * tile]
    element = at * tile + lax.broadcasted_iota(jnp.int32, ids.shape, 1)
    return jnp.where(element < live[0], ids, -1)


def fill_gather(hot, conn, blocks, bases, tile):
    row = 0
    for at, block in enumerate(blocks):
        size = block.shape[1]
        iota = lax.broadcasted_iota(jnp.int32, (size, tile), 0)
        for corner in range(6):
            hot[row : row + size, corner * tile : (corner + 1) * tile] = one_hot(
                iota, conn[corner : corner + 1, :] - bases[at]
            )
        row += size


def fill_values(values, blocks):
    column = 0
    for block in blocks:
        size = block.shape[1]
        values[:, column : column + size] = split_rows(block[...])
        column += size


def magnetic_terms_kernel(places, mode_dev, live, conn, stiffness, mass_r, *refs):
    *blocks, slab = views(places, refs)
    out, slab_part, done, values, hots, operator, slab_values, slab_hots = refs[-8:]
    tile = operator.shape[2]
    fill_values(slab_values, (slab,))
    done[...] = jnp.zeros_like(done)
    fill_values(values, blocks)
    bases = [0]
    for block in blocks[:-1]:
        bases.append(bases[-1] + block.shape[1])
    lane = lax.broadcasted_iota(jnp.int32, (8, tile), 0)
    squares = (own_member() * mode_dev + lax.rem(lane, mode_dev)).astype(f32) ** 2
    for step in range(out.shape[0]):
        hot = hots.at[step % 2]
        ids = tile_ids(conn, live, step, tile)
        slab_hot = slab_hots.at[step % 2]
        fill_gather(slab_hot, ids, (slab,), (base_of(0, slab.shape[1]),), tile)
        slab_part[step] = halves_sum(
            jnp.dot(slab_values[...], slab_hot[...], preferred_element_type=f32)
        )
        ids = by_partner(ids, bases[1], blocks[1].shape[1])
        fill_gather(hot, ids, blocks, bases, tile)
        got = halves_sum(jnp.dot(values[...], hot[...], preferred_element_type=f32))
        at = slice(step * tile, (step + 1) * tile)
        for a in range(6):
            for b in range(6):
                operator[a * 6 + b] = diffusivity * (
                    stiffness[a, b : b + 1, at] + squares * mass_r[a, b : b + 1, at]
                )
        for low in range(0, out.shape[1], 8):
            for a in range(6):
                total = None
                for b in range(6):
                    term = operator[a * 6 + b] * got[low : low + 8, b * tile : (b + 1) * tile]
                    total = term if total is None else total + term
                out[step, low : low + 8, a * tile : (a + 1) * tile] = total


def magnetic_terms(blocks, slab, mode_dev, live, conn, stiffness, mass_r, after):
    rows = blocks[0].shape[0]
    elems = conn.shape[1]
    tile = ELEM_TILE
    total = sum(block.shape[1] for block in blocks)
    given, places = operands(blocks + [slab])
    return pl.pallas_call(
        functools.partial(magnetic_terms_kernel, places, mode_dev),
        in_specs=[smem] + [vmem] * (3 + len(given)) + [anywhere] * len(after),
        out_shape=[
            jax.ShapeDtypeStruct((elems // tile, rows, 6 * tile), f32),
            jax.ShapeDtypeStruct((elems // tile, rows, 6 * tile), f32),
            jax.ShapeDtypeStruct((8, 128), f32),
        ],
        scratch_shapes=[
            pltpu.VMEM((2 * rows, total), bf16),
            pltpu.VMEM((2, total, 6 * tile), bf16),
            pltpu.VMEM((36, 8, tile), f32),
            pltpu.VMEM((2 * rows, slab.shape[1]), bf16),
            pltpu.VMEM((2, slab.shape[1], 6 * tile), bf16),
        ],
        compiler_params=params(28 << 20),
        cost_estimate=cost(30),
        name="magnetic_terms",
    )(live, conn, stiffness, mass_r, *given, *after)


def gather_kernel(places, steps, live, conn, earlier, *refs):
    blocks = views(places, refs)
    out, values, hots = refs[-3:]
    tile = out.shape[2] // 6
    fill_values(values, blocks)
    bases = [base_of(step, block.shape[1]) for step, block in zip(steps, blocks)]
    for step in range(out.shape[0]):
        hot = hots.at[step % 2]
        fill_gather(hot, tile_ids(conn, live, step, tile), blocks, bases, tile)
        out[step] = earlier[step] + halves_sum(
            jnp.dot(values[...], hot[...], preferred_element_type=f32)
        )


def gathered(blocks, steps, live, conn, earlier):
    rows = blocks[0].shape[0]
    elems = conn.shape[1]
    tile = ELEM_TILE
    total = sum(block.shape[1] for block in blocks)
    given, places = operands(blocks)
    return pl.pallas_call(
        functools.partial(gather_kernel, places, steps),
        in_specs=[smem] + [vmem] * (2 + len(given)),
        out_shape=jax.ShapeDtypeStruct((elems // tile, rows, 6 * tile), f32),
        scratch_shapes=[
            pltpu.VMEM((2 * rows, total), bf16),
            pltpu.VMEM((2, total, 6 * tile), bf16),
        ],
        compiler_params=params(28 << 20),
        cost_estimate=cost(5),
        name="gathered",
    )(live, conn, earlier, *given)


def fill_scatter(hot, conn_columns, first, tile):
    iota = lax.broadcasted_iota(jnp.int32, (tile, hot.shape[1]), 1)
    for corner in range(6):
        hot[corner * tile : (corner + 1) * tile, :] = one_hot(
            iota, conn_columns[:, corner : corner + 1] - first
        )


def ghost_hot_kernel(first, live, conn, by_slot, by_corner):
    slots, tile = by_slot.shape[1], by_slot.shape[2] // 6
    for step in range(by_slot.shape[0]):
        ids = by_partner(tile_ids(conn, live, step, tile), first, slots // 2)
        iota = lax.broadcasted_iota(jnp.int32, (slots, tile), 0)
        for corner in range(6):
            by_slot[step, :, corner * tile : (corner + 1) * tile] = one_hot(
                iota, ids[corner : corner + 1, :] - first
            )
        fill_scatter(by_corner.at[step], columns_of(ids), first, tile)


def ghost_hot(first, slots, live, conn):
    wide = 6 * ELEM_TILE
    steps = conn.shape[1] // ELEM_TILE
    return pl.pallas_call(
        functools.partial(ghost_hot_kernel, first),
        in_specs=[smem, vmem],
        out_shape=[
            jax.ShapeDtypeStruct((steps, slots, wide), bf16),
            jax.ShapeDtypeStruct((steps, wide, slots), bf16),
        ],
        compiler_params=params(),
        cost_estimate=cost(3),
        name="ghost_hot",
    )(live, conn)


def ghost_terms_kernel(
    hots, hots_columns, coupling, magnetic_part, electric_part, left, right,
    terms, left_sums, right_sums, values
):
    tile = terms.shape[2] // 6
    rows, cap = left.shape
    fill_values(values, (left, right))
    sums = None
    for step in range(terms.shape[0]):
        got = electric_part[step] + halves_sum(
            jnp.dot(values[...], hots[step], preferred_element_type=f32)
        )
        across = slice(step * tile, (step + 1) * tile)
        for low in range(0, rows, 16):
            for a in range(6):
                at = slice(a * tile, (a + 1) * tile)
                total = -magnetic_part[step, low : low + 16, at]
                for b in range(6):
                    total = total + coupling[a, b : b + 1, across] * got[low : low + 16, b * tile : (b + 1) * tile]
                high = total.astype(bf16)
                terms[step, low : low + 16, at] = high
                terms[step, rows + low : rows + low + 16, at] = (total - high.astype(f32)).astype(bf16)
        part = halves_sum(jnp.dot(terms[step], hots_columns[step], preferred_element_type=f32))
        if step == 0:
            left_sums[...] = part[:, :cap]
            right_sums[...] = part[:, cap:]
        else:
            left_sums[...] += part[:, :cap]
            right_sums[...] += part[:, cap:]


def ghost_terms(hots, coupling, magnetic_part, electric_part, left, right):
    rows, cap = left.shape
    steps, _, wide = electric_part.shape
    return pl.pallas_call(
        ghost_terms_kernel,
        in_specs=[vmem] * 7,
        out_shape=[
            jax.ShapeDtypeStruct((steps, 2 * rows, wide), bf16),
            jax.ShapeDtypeStruct((rows, cap), f32),
            jax.ShapeDtypeStruct((rows, cap), f32),
        ],
        scratch_shapes=[pltpu.VMEM((2 * rows, 2 * cap), bf16)],
        compiler_params=params(),
        cost_estimate=cost(8),
        name="ghost_terms",
    )(*hots, coupling, magnetic_part, electric_part, left, right)


def own_sums_kernel(live, conn, terms, out, hots):
    tile = terms.shape[2] // 6
    for step in range(terms.shape[0]):
        hot = hots.at[step % 2]
        fill_scatter(hot, columns_of(tile_ids(conn, live, step, tile)), 0, tile)
        part = halves_sum(jnp.dot(terms[step], hot[...], preferred_element_type=f32))
        if step == 0:
            out[...] = part
        else:
            out[...] += part


def own_sums(live, conn, terms, nodes):
    rows, wide = terms.shape[1] // 2, terms.shape[2]
    return pl.pallas_call(
        own_sums_kernel,
        in_specs=[smem, vmem, vmem],
        out_shape=jax.ShapeDtypeStruct((rows, nodes), f32),
        scratch_shapes=[pltpu.VMEM((2, wide, nodes), bf16)],
        compiler_params=params(),
        cost_estimate=cost(9),
        name="own_sums",
    )(live, conn, terms)


def interface_hot_kernel(steps, counts, interface, by_slot, by_node):
    ids = interface_ids(interface, counts)
    iota = lax.broadcasted_iota(jnp.int32, by_slot.shape, 1)
    by_slot[...] = one_hot(iota, columns_of(ids)[:, :1])
    member_hot(by_node, ids, steps, by_node.shape[0] // len(steps))


def interface_hot(counts, interface, nodes, steps):
    slots = interface.shape[1]
    return pl.pallas_call(
        functools.partial(interface_hot_kernel, steps),
        in_specs=[smem, vmem],
        out_shape=[
            jax.ShapeDtypeStruct((slots, nodes), bf16),
            jax.ShapeDtypeStruct((nodes, slots), bf16),
        ],
        compiler_params=params(),
        cost_estimate=cost(2),
        name="interface_hot",
    )(counts, interface)


def finish_kernel(hot, magnetic, sums, left, right, inv_mass, out, parts, sems):
    values = jnp.concatenate([split_rows(left[...]), split_rows(right[...])], 1)
    count, _, width = parts.shape
    copies = []
    for part in range(count):
        at = slice(part * width, (part + 1) * width)
        extra = halves_sum(jnp.dot(values, hot[:, at], preferred_element_type=f32))
        parts[part] = magnetic[:, at] + time_step * inv_mass[:, at] * (sums[:, at] + extra)
        copies.append(pltpu.make_async_copy(parts.at[part], out.at[:, at], sems.at[part]))
        copies[-1].start()
    for copy in copies:
        copy.wait()


def finish(hot, magnetic, sums, left, right, inv_mass):
    rows, nodes = magnetic.shape
    count = 4
    return pl.pallas_call(
        finish_kernel,
        in_specs=[vmem] * 6,
        out_specs=anywhere,
        out_shape=jax.ShapeDtypeStruct((rows, nodes), f32),
        scratch_shapes=[
            pltpu.VMEM((count, rows, nodes // count), f32),
            pltpu.SemaphoreType.DMA((count,)),
        ],
        compiler_params=params(),
        cost_estimate=cost(2),
        name="finish",
    )(hot, magnetic, sums, left, right, inv_mass)


def between_chips(blocks):
    members = lax.axis_size("mode")
    order = sorted(range(1, members // 2), key=lambda t: -t)
    got = {
        t: lax.ppermute(blocks[t], "mode", [(k, k ^ (2 * t)) for k in range(members)])
        for t in order
    }
    return [blocks[0]] + [got[t] for t in range(1, members // 2)]


def between_cores(blocks, after):
    members = lax.axis_size("mode")
    return lax.ppermute(lower_halves(blocks, after), "mode", [(k, k ^ 1) for k in range(members)])


def neighbours(one, two):
    count = lax.axis_size("mesh")
    got = []
    for values, start in ((one, 0), (two, 1)):
        lower = range(start, count - 1, 2)
        pairs = [(i, i + 1) for i in lower] + [(i + 1, i) for i in lower]
        got.append(lax.ppermute(values, "mesh", pairs))
    return got


def on_device(
    magnetic, velocity, stiffness, mass_r, coupling, inv_mass, connect, interface, counts, elem_live
):
    fields, vector_parts, mode_dev, node_dev = magnetic.shape
    rows = fields * vector_parts * mode_dev
    cap = interface.shape[1] // 2
    members = lax.axis_size("mode")
    slab = node_dev // members
    values = magnetic.reshape(rows, node_dev)

    far = pack(values, tuple(range(2, members // 2)), slab, ())
    near = pack(values, (0, 1), slab, (far[0],))
    packed = near + far
    kept = between_chips(packed)
    own = Block(values, rows)
    mag_left, mag_right = neighbours(
        *interface_values([own], (None,), counts, interface, 1, (packed[0],))
    )
    extended = [own, Block(mag_left, rows), Block(mag_right, rows)]
    steps = tuple(range(members))
    hot, node_hot = interface_hot(counts, interface, node_dev, steps)
    ghost_hots = ghost_hot(node_dev, 2 * cap, elem_live, connect)
    swapped = between_cores(kept, (mag_left, mag_right, hot, ghost_hots[0]))
    arrived = []
    for t, block in enumerate(kept):
        arrived += [Block(block, rows), Block(swapped, rows, t)]
    inverse, forward = transform_tables(mode_dev, members)
    sent = list(transform(arrived, velocity, inverse, forward, mode_dev, fields))
    sent[1] = relay(sent[1], (sent[2],))
    kept = between_chips(sent)
    magnetic_part, slab_part, done = magnetic_terms(
        extended, Block(sent[0], rows), mode_dev, elem_live, connect, stiffness, mass_r, (sent[1],)
    )
    electric = []
    swapped = between_cores(kept[:2], (done,))
    for t, block in enumerate(kept[:2]):
        electric += [Block(block, rows), Block(swapped, rows, t)]
    swapped = between_cores(kept[2:], ())
    for t, block in enumerate(kept[2:]):
        electric += [Block(block, rows), Block(swapped, rows, t)]
    ele_left, ele_right = neighbours(*picked(electric, node_hot))
    electric_part = gathered(electric[1:], steps[1:], elem_live, connect, slab_part)
    terms, left_sums, right_sums = ghost_terms(
        ghost_hots, coupling, magnetic_part, electric_part, ele_left, ele_right
    )
    sum_left, sum_right = neighbours(left_sums, right_sums)
    sums = own_sums(elem_live, connect, terms, node_dev)
    out = finish(hot, values, sums, sum_left, sum_right, inv_mass[None, :])
    return out.reshape(magnetic.shape)


def solution(mesh):
    return jax.shard_map(
        on_device,
        mesh=mesh,
        in_specs=(
            P(None, None, "mode", "mesh"),
            P(None, None, ("mesh", "mode")),
            P(None, None, "mesh"),
            P(None, None, "mesh"),
            P(None, None, "mesh"),
            P("mesh"),
            P(None, "mesh"),
            P("mesh", None),
            P("mesh", None),
            P("mesh"),
        ),
        out_specs=P(None, None, "mode", "mesh"),
        check_vma=False,
    )
```
